32 devices in a mesh: gx: 2 (over y), gy: 4 (over x, core), gz: 4 (over z).
Axes of the slice: x: 2, y: 2, z: 4, core: 2. Of those that a mesh axis runs over, the one named last changes fastest.
Arguments:
- features: bfloat16 [24576, 256], P(('gx', 'gy', 'gz')), may hold values from -6 to 6
- tile_values: bfloat16 [256, 8, 128, 128], P(('gx', 'gy', 'gz')), as said below
- tile_columns: int32 [256, 8], P(('gx', 'gy', 'gz')), may hold values from 0 to 7
- tile_present: int32 [256, 8], P(('gx', 'gy', 'gz')), may hold values 0 or 1
- host_root: int32 [64], P(('gx', 'gy')), may hold values from 0 to 3, as said below
- host_block: int32 [64], P(('gx', 'gy')), may hold values from 0 to 1
- self_one: bfloat16 [256, 256], replicated, may hold values from -0.375 to 0.375
- neigh_one: bfloat16 [256, 256], replicated, may hold values from -0.375 to 0.375
- scale_one: float32 [256], replicated, may hold values from 0.25 to 1.75
- shift_one: float32 [256], replicated, may hold values from -3 to 3
- self_two: bfloat16 [256, 256], replicated, may hold values from -0.375 to 0.375
- neigh_two: bfloat16 [256, 256], replicated, may hold values from -0.375 to 0.375
Outputs:
- embedding: bfloat16 [24576, 256], P(('gx', 'gy', 'gz'))
The draws below stay inside these ranges and needn't reach their ends.
Inputs may be any that keep to these rules, and one draw needn't show every extreme that they name: `host_root`: never the holder's own gz index; the 2 replica slots of one device name 2 different devices. `tile_values`: entries lie in 0 to 1.8 / sqrt(1024).
All inputs are finite; a program needn't handle non-finite values. No bound on the sum of `tile_present` on one device may be relied on, other than what follows from the above.
Results may differ from the reference program's by a relative error of at most 0.012.
Values may be sent and summed in bfloat16 or wider, within the bound.
A program may use at most 64 MiB of HBM per device.

```python
import math
import jax
import jax.numpy as jnp
from jax import lax

F = 256
TILE = 128
K = 8
OWN = 4
SPLIT = 2
HOST = 2
SLOTS = 8
VERTICES = 24576
N_GZ = 4
DEVICES = 32


def draw_tile_values(key, part):
    shape = (DEVICES * (OWN + SPLIT + HOST), K, TILE, TILE)
    present = jax.random.uniform(jax.random.fold_in(key, 1), shape) < 0.4
    size = jax.random.uniform(jax.random.fold_in(key, 2), shape, minval=0.5, maxval=1.5)
    values = jnp.where(present, size, 0.0) * (1.2 / math.sqrt(K * TILE))
    return values.astype(jnp.float32).astype(jnp.bfloat16)


def host_tables(key):
    scores = jax.random.randint(jax.random.fold_in(key, 11), (DEVICES, N_GZ - 1), 0, 1 << 20)
    scores = scores * N_GZ + jnp.arange(N_GZ - 1, dtype=jnp.int32)[None, :]
    picked = jnp.argsort(scores, axis=1)[:, :HOST].astype(jnp.int32)
    own = (jnp.arange(DEVICES, dtype=jnp.int32) % N_GZ)[:, None]
    roots = (own + 1 + picked) % N_GZ
    blocks = jax.random.randint(jax.random.fold_in(key, 12), (DEVICES, HOST), 0, SPLIT)
    return (roots.reshape(-1).astype(jnp.int32), blocks.reshape(-1).astype(jnp.int32))


def draw_host_root(key, part):
    return host_tables(key)[0]


def draw_host_block(key, part):
    return host_tables(key)[1]


def set_ends(drawn, rng, least, high):
    longest = drawn.shape.index(max(drawn.shape))
    spots = []
    for shift in (0, 1):
        where = [jax.random.randint(jax.random.fold_in(rng, axis), (), 0, length) for axis, length in enumerate(drawn.shape)]
        where[longest] = (where[longest] + shift) % drawn.shape[longest]
        spots.append(tuple(where))
    return drawn.at[spots[0]].set(least).at[spots[1]].set(high)


def steps_of(rng, dims, split, smallest, high):
    gain, own = 1.0, jax.random.fold_in(rng, 6)
    for axis_at, blocks in split:
        draws = jnp.exp(jax.random.uniform(jax.random.fold_in(own, axis_at), (blocks,), jnp.float32, smallest / len(split), high / len(split)))
        gain = gain * jnp.repeat(draws, dims[axis_at] // blocks).reshape([-1 if axis == axis_at else 1 for axis in range(len(dims))])
    return gain


def gaussian(rng, extent, deviation, reach, split=(), kind=jnp.bfloat16):
    array = deviation * jax.random.normal(rng, extent, jnp.float32)
    if split:
        array = array * steps_of(rng, extent, split, -0.22, 0.18)
    return jnp.clip(array, -reach, reach).astype(kind)


def setup_inputs(seed: int = 0) -> dict:
    seeds = jax.random.split(jax.random.key(seed), 13)
    return {
        "features": gaussian(seeds[0], (VERTICES, F), 1.0, 6.0, ((0, 32),)),
        "tile_values": draw_tile_values(jax.random.fold_in(seeds[12], 71), 0),
        "tile_columns": set_ends(jax.random.randint(seeds[2], (DEVICES * SLOTS, K), 0, SLOTS), jax.random.fold_in(seeds[2], 1), 0, SLOTS - 1).astype(jnp.int32),
        "tile_present": set_ends((jax.random.randint(seeds[3], (DEVICES * SLOTS, K), 0, 4) < 3).astype(jnp.int32), jax.random.fold_in(seeds[3], 1), 0, 1),
        "host_root": draw_host_root(jax.random.fold_in(seeds[12], 71), 0),
        "host_block": draw_host_block(jax.random.fold_in(seeds[12], 71), 0),
        "self_one": gaussian(seeds[6], (F, F), F ** -0.5, 0.375),
        "neigh_one": gaussian(seeds[7], (F, F), F ** -0.5, 0.375),
        "scale_one": jnp.clip(1.0 + 0.15 * jax.random.normal(seeds[8], (F,), jnp.float32), 0.25, 1.75),
        "shift_one": gaussian(seeds[9], (F,), 0.5, 3.0, (), jnp.float32),
        "self_two": gaussian(seeds[10], (F, F), F ** -0.5, 0.375),
        "neigh_two": gaussian(seeds[11], (F, F), F ** -0.5, 0.375),
    }


def aggregate(view, tile_values, tile_columns, tile_present):

    def one_device(items):
        held, tiles, columns, present = items
        picked = held[columns]
        picked = jnp.where(present[:, :, None, None] > 0, picked, jnp.zeros_like(picked))
        return jnp.einsum('bkij,bkjf->bif', tiles.astype(jnp.float32), picked.astype(jnp.float32))
    return lax.map(one_device, (view, tile_values, tile_columns, tile_present))

def layer(rows, tile_values, tile_columns, tile_present, host_root, host_block, w_self, w_neigh):
    rooted = rows.reshape(DEVICES, OWN + SPLIT, TILE, F)
    sender = jnp.repeat(jnp.arange(DEVICES, dtype=jnp.int32), HOST)
    base = sender // N_GZ * N_GZ
    source = ((base + host_root) * (OWN + SPLIT) + OWN + host_block).astype(jnp.int32)
    hosted = rows.reshape(DEVICES * (OWN + SPLIT), TILE, F)[source].reshape(DEVICES, HOST, TILE, F)
    view = jnp.concatenate([rooted, hosted], axis=1)
    tiles = tile_values.reshape(DEVICES, OWN + SPLIT + HOST, K, TILE, TILE)
    columns = tile_columns.reshape(DEVICES, OWN + SPLIT + HOST, K)
    present = tile_present.reshape(DEVICES, OWN + SPLIT + HOST, K)
    partial_value = aggregate(view, tiles, columns, present)
    sent = partial_value[:, OWN + SPLIT:].astype(jnp.bfloat16)
    sent = lax.optimization_barrier(sent).astype(jnp.float32).reshape(DEVICES * HOST, TILE, F)
    target = ((base + host_root) * SPLIT + host_block).astype(jnp.int32)
    remote = jax.ops.segment_sum(sent, target, num_segments=DEVICES * SPLIT).reshape(DEVICES, SPLIT, TILE, F)
    total = partial_value[:, :OWN + SPLIT].at[:, OWN:].add(remote)
    neighbours = total.astype(jnp.bfloat16).reshape(-1, F)
    return jnp.dot(rows, w_self, preferred_element_type=jnp.float32) + jnp.dot(neighbours, w_neigh, preferred_element_type=jnp.float32)

def reference(features, tile_values, tile_columns, tile_present, host_root, host_block, self_one, neigh_one, scale_one, shift_one, self_two, neigh_two):
    first = layer(features, tile_values, tile_columns, tile_present, host_root, host_block, self_one, neigh_one)
    count = first.shape[0]
    mean = lax.optimization_barrier(jnp.sum(first, axis=0)) / count
    meansq = lax.optimization_barrier(jnp.sum(first * first, axis=0)) / count
    var = meansq - mean * mean
    hidden = jax.nn.relu((first - mean) * lax.rsqrt(var + 1e-05) * scale_one + shift_one).astype(jnp.bfloat16)
    second = layer(hidden, tile_values, tile_columns, tile_present, host_root, host_block, self_two, neigh_two)
    return second.astype(jnp.bfloat16)
```

```python
import functools

import jax
import jax.numpy as jnp
from jax import lax
from jax.experimental import pallas as pl
from jax.experimental.pallas import tpu as pltpu
from jax.sharding import PartitionSpec as P

OWN = 4
SPLIT = 2
LANES = 128
F32 = jnp.float32
BF16 = jnp.bfloat16


def dot(a, b):
    return jnp.dot(a, b, preferred_element_type=F32)


def kernel(
    sizes,
    columns_ref,
    present_ref,
    root_ref,
    block_ref,
    features_hbm,
    tiles_hbm,
    self_one_hbm,
    neigh_one_hbm,
    self_two_hbm,
    neigh_two_hbm,
    scale_ref,
    shift_ref,
    out_ref,
    *scratch,
):
    nx, ny, group, slots, ks, tile, width, rooted = sizes
    hosts = slots - rooted
    rows_n = rooted * tile
    own_n = OWN * tile
    parts = width // LANES
    peers = group - 1
    scratch = list(scratch)

    def take(n):
        got = scratch[:n]
        del scratch[:n]
        return got

    feat, tiles, ws1, wn1, ws2, wn2 = take(6)
    dense, acc, first, hidden, delta = take(5)
    hosted = take(parts)
    replica = take(parts)
    f_in = [take(parts) for _ in range(2)]
    f_out = [take(parts) for _ in range(2)]
    p_in = [take(parts) for _ in range(2)]
    p_out = [take(parts) for _ in range(2)]
    z_out, z_in, xy_out, xy_in = take(4)
    local_sem, f_send, f_recv, p_send, p_recv, z_send, z_recv, xy_send, xy_recv = take(9)

    gx, gy, gz = lax.axis_index("gx"), lax.axis_index("gy"), lax.axis_index("gz")
    loads = [
        pltpu.make_async_copy(src, dst, local_sem.at[i])
        for i, (src, dst) in enumerate(
            zip(
                (features_hbm, tiles_hbm, self_one_hbm, neigh_one_hbm, self_two_hbm, neigh_two_hbm),
                (feat, tiles, ws1, wn1, ws2, wn2),
            )
        )
    ]
    for load in loads:
        load.start()

    def ahead(j):
        return lax.rem(gz + j, group)

    def behind(j):
        return lax.rem(gz + group - j, group)

    spots = [(i, k) for i in range(nx) for k in range(ny) if (i, k) != (0, 0)]

    def spot_id(spot):
        return {"gx": lax.rem(gx + spot[0], nx), "gy": lax.rem(gy + spot[1], ny)}

    barrier = pltpu.get_barrier_semaphore()
    for j in range(1, group):
        pl.semaphore_signal(
            barrier, inc=1, device_id={"gz": ahead(j)}, device_id_type=pl.DeviceIdType.MESH
        )
    for spot in spots:
        pl.semaphore_signal(
            barrier, inc=1, device_id=spot_id(spot), device_id_type=pl.DeviceIdType.MESH
        )

    def z_copy(src, dst, send, recv, j):
        return pltpu.make_async_remote_copy(
            src_ref=src,
            dst_ref=dst,
            send_sem=send,
            recv_sem=recv,
            device_id={"gz": ahead(j)},
            device_id_type=pl.DeviceIdType.MESH,
        )

    def f_copy(l, c, j):
        return z_copy(
            f_out[l][c].at[j - 1], f_in[l][c].at[j - 1], f_send.at[l, c, j - 1], f_recv.at[l, c, j - 1], j
        )

    def p_copy(l, c, j):
        return z_copy(
            p_out[l][c].at[j - 1], p_in[l][c].at[j - 1], p_send.at[l, c, j - 1], p_recv.at[l, c, j - 1], j
        )

    def zs_copy(j):
        return z_copy(z_out, z_in.at[j - 1], z_send.at[j - 1], z_recv.at[j - 1], j)

    def xy_copy(n):
        return pltpu.make_async_remote_copy(
            src_ref=xy_out,
            dst_ref=xy_in.at[n],
            send_sem=xy_send.at[n],
            recv_sem=xy_recv.at[n],
            device_id=spot_id(spots[n]),
            device_id_type=pl.DeviceIdType.MESH,
        )

    def lanes(c):
        return slice(c * LANES, (c + 1) * LANES)

    def wanted(j):
        q = ahead(j)
        sel = jnp.int32(0)
        for h in range(hosts):
            at = q * hosts + h
            sel = jnp.where(root_ref[at] == gz, block_ref[at], sel)
        return sel

    def spread(l, source, base):
        for c in range(parts):
            for j in range(1, group):
                f_out[l][c][j - 1] = source[base + wanted(j)][:, lanes(c)]
                f_copy(l, c, j).start()

    loads[0].wait()
    pl.semaphore_wait(barrier, peers + len(spots))
    spread(0, feat, OWN)

    loads[1].wait()

    def build(b, carry):
        at = pl.multiple_of(b * tile, tile)
        for c in range(slots):
            total = jnp.zeros((tile, tile), BF16)
            for k in range(ks):
                on = (columns_ref[b, k] == c) & (present_ref[b, k] > 0)
                total = total + jnp.where(on, tiles[b, k], jnp.zeros((tile, tile), BF16))
            dense[pl.ds(at, tile), c * tile : (c + 1) * tile] = total
        return carry

    lax.fori_loop(0, slots, build, 0)
    for load in loads[2:]:
        load.wait()

    def blocks_of(n):
        return 2 * tile if n % (2 * tile) == 0 else tile

    def layer(l, rows, hosted_block, w_self, w_neigh, emit):
        flat = rows.reshape(rows_n, width)
        step = blocks_of(slots * tile)

        def local(i, carry):
            at = pl.multiple_of(i * step, step)
            acc[pl.ds(at, step), :] = dot(dense[pl.ds(at, step), 0:rows_n], flat[...])
            return carry

        lax.fori_loop(0, slots * tile // step, local, 0)

        for c in range(parts):
            for j in range(1, group):
                f_copy(l, c, j).wait_recv()
            for h in range(hosts):
                root = root_ref[gz * hosts + h]
                at = jnp.maximum(lax.rem(gz - root + group, group) - 1, 0)
                hosted[c][h * tile : (h + 1) * tile, :] = hosted_block(f_in[l][c][at], at, c)
            part = acc[rows_n:, lanes(c)] + dot(dense[rows_n:, rows_n:], hosted[c][...])
            replica[c][...] = part.astype(BF16).reshape(hosts, tile, LANES)
            for j in range(1, group):
                target = ahead(j)
                sel = jnp.int32(0)
                for h in range(hosts):
                    sel = jnp.where(root_ref[gz * hosts + h] == target, h, sel)
                p_out[l][c][j - 1] = replica[c][sel]
                p_copy(l, c, j).start()

        own_step = blocks_of(own_n)
        split_n = rows_n - own_n

        def with_hosted(at, n):
            return jnp.concatenate(
                [
                    acc[pl.ds(at, n), lanes(c)] + dot(dense[pl.ds(at, n), rows_n:], hosted[c][...])
                    for c in range(parts)
                ],
                axis=1,
            )

        def own(i, carry):
            at = pl.multiple_of(i * own_step, own_step)
            neighbours = with_hosted(at, own_step).astype(BF16)
            emit(
                pl.ds(at, own_step),
                dot(flat[pl.ds(at, own_step), :], w_self[...]) + dot(neighbours, w_neigh[...]),
            )
            return carry

        lax.fori_loop(0, own_n // own_step, own, 0)
        acc[own_n:rows_n, :] = with_hosted(own_n, split_n)
        selfs = dot(flat[own_n:rows_n, :], w_self[...])

        for c in range(parts):
            for j in range(1, group):
                p_copy(l, c, j).wait_recv()
            for s in range(SPLIT):
                at = own_n + s * tile
                total = acc[at : at + tile, lanes(c)]
                for j in range(1, group):
                    q = behind(j)
                    count = jnp.int32(0)
                    for h in range(hosts):
                        spot = q * hosts + h
                        count = count + jnp.where(
                            (root_ref[spot] == gz) & (block_ref[spot] == s), 1, 0
                        )
                    total = total + count.astype(F32) * p_in[l][c][j - 1].astype(F32)
                acc[at : at + tile, lanes(c)] = total
        emit(slice(own_n, rows_n), selfs + dot(acc[own_n:rows_n, :].astype(BF16), w_neigh[...]))

    def keep(at, value):
        first[at, :] = value

    layer(0, feat, lambda block, at, c: block, ws1, wn1, keep)

    value = first[...]
    sums = jnp.sum(value, axis=0, keepdims=True)
    squares = jnp.sum(value * value, axis=0, keepdims=True)
    z_out[...] = jnp.concatenate([sums, squares, jnp.zeros((6, width), F32)], axis=0)
    for j in range(1, group):
        zs_copy(j).start()
    center = sums * (1.0 / rows_n)
    delta[...] = (first[own_n:rows_n, :] - center).astype(BF16).reshape(SPLIT, tile, width)
    spread(1, delta, 0)

    total = z_out[...]
    for j in range(1, group):
        zs_copy(j).wait_recv()
        total = total + z_in[j - 1]
    xy_out[...] = total
    for n in range(len(spots)):
        xy_copy(n).start()
    for n in range(len(spots)):
        xy_copy(n).wait_recv()
        total = total + xy_in[n]
    count = rows_n * nx * ny * group
    mean = total[0:1, :] / count
    var = total[1:2, :] / count - mean * mean
    gain = lax.rsqrt(var + 1e-05) * scale_ref[...]
    shift = shift_ref[...]

    hidden[...] = (
        jnp.maximum((first[...] - mean) * gain + shift, 0.0)
        .astype(BF16)
        .reshape(rooted, tile, width)
    )

    def normal(block, at, c):
        middle = z_in[at][0:1, lanes(c)] * (1.0 / rows_n)
        moved = block.astype(F32) + (middle - mean[:, lanes(c)])
        return jnp.maximum(moved * gain[:, lanes(c)] + shift[:, lanes(c)], 0.0).astype(BF16)

    def finish(at, value):
        out_ref[at, :] = value.astype(BF16)

    layer(1, hidden, normal, ws2, wn2, finish)

    for l in range(2):
        for c in range(parts):
            for j in range(1, group):
                f_copy(l, c, j).wait_send()
                p_copy(l, c, j).wait_send()
    for j in range(1, group):
        zs_copy(j).wait_send()
    for n in range(len(spots)):
        xy_copy(n).wait_send()


def per_device(
    features,
    tile_values,
    tile_columns,
    tile_present,
    host_root,
    host_block,
    self_one,
    neigh_one,
    scale_one,
    shift_one,
    self_two,
    neigh_two,
):
    slots, ks, tile, _ = tile_values.shape
    width = features.shape[1]
    rooted = features.shape[0] // tile
    hosts = slots - rooted
    nx, ny, group = (lax.axis_size(name) for name in ("gx", "gy", "gz"))
    peers, spots = group - 1, nx * ny - 1
    parts = width // LANES
    rows_n = rooted * tile
    sizes = (nx, ny, group, slots, ks, tile, width, rooted)

    box = pltpu.VMEM((peers, tile, LANES), BF16)
    dma = pltpu.SemaphoreType.DMA
    scratch = [
        pltpu.VMEM((rooted, tile, width), BF16),
        pltpu.VMEM(tile_values.shape, BF16),
        *[pltpu.VMEM((width, width), BF16)] * 4,
        pltpu.VMEM((slots * tile, slots * tile), BF16),
        pltpu.VMEM((slots * tile, width), F32),
        pltpu.VMEM((rows_n, width), F32),
        pltpu.VMEM((rooted, tile, width), BF16),
        pltpu.VMEM((SPLIT, tile, width), BF16),
        *[pltpu.VMEM((hosts * tile, LANES), BF16)] * parts,
        *[pltpu.VMEM((hosts, tile, LANES), BF16)] * parts,
        *[box] * (8 * parts),
        pltpu.VMEM((8, width), F32),
        pltpu.VMEM((peers, 8, width), F32),
        pltpu.VMEM((8, width), F32),
        pltpu.VMEM((spots, 8, width), F32),
        dma((6,)),
        *[dma((2, parts, peers))] * 4,
        *[dma((peers,))] * 2,
        *[dma((spots,))] * 2,
    ]
    smem = pl.BlockSpec(memory_space=pltpu.SMEM)
    vmem = pl.BlockSpec(memory_space=pltpu.VMEM)
    anywhere = pl.BlockSpec(memory_space=pl.ANY)
    return pl.pallas_call(
        functools.partial(kernel, sizes),
        out_shape=jax.ShapeDtypeStruct((rows_n, width), BF16),
        in_specs=[smem] * 4 + [anywhere] * 6 + [vmem] * 2,
        out_specs=vmem,
        scratch_shapes=scratch,
        compiler_params=pltpu.CompilerParams(
            collective_id=0, has_side_effects=True, vmem_limit_bytes=40 * 1024 * 1024
        ),
    )(
        tile_columns,
        tile_present,
        host_root,
        host_block,
        features.reshape(rooted, tile, width),
        tile_values,
        self_one,
        neigh_one,
        self_two,
        neigh_two,
        scale_one.reshape(1, width),
        shift_one.reshape(1, width),
    )


def solution(mesh):
    return jax.shard_map(
        per_device,
        mesh=mesh,
        in_specs=(
            P(("gx", "gy", "gz"), None),
            P(("gx", "gy", "gz"), None, None, None),
            P(("gx", "gy", "gz"), None),
            P(("gx", "gy", "gz"), None),
            P(("gx", "gy")),
            P(("gx", "gy")),
            P(),
            P(),
            P(),
            P(),
            P(),
            P(),
        ),
        out_specs=P(("gx", "gy", "gz"), None),
        check_vma=False,
    )
```

```python
import functools

import jax
import jax.numpy as jnp
from jax import lax
from jax.experimental import pallas as pl
from jax.experimental.pallas import tpu as pltpu
from jax.sharding import PartitionSpec as P

OWN = 4
SPLIT = 2
LANES = 128
F32 = jnp.float32
BF16 = jnp.bfloat16


def dot(a, b):
    return jnp.dot(a, b, preferred_element_type=F32)


def kernel(
    sizes,
    columns_hbm,
    present_hbm,
    root_hbm,
    block_hbm,
    features_hbm,
    tiles_hbm,
    self_one_hbm,
    neigh_one_hbm,
    self_two_hbm,
    neigh_two_hbm,
    scale_hbm,
    shift_hbm,
    out_ref,
    *scratch,
):
    nx, ny, group, slots, ks, tile, width, rooted = sizes
    hosts = slots - rooted
    rows_n = rooted * tile
    own_n = OWN * tile
    parts = width // LANES
    peers = group - 1
    scratch = list(scratch)

    def take(n):
        got = scratch[:n]
        del scratch[:n]
        return got

    columns_ref, present_ref, root_ref, block_ref = take(4)
    feat, tiles, ws1, wn1, ws2, wn2, scale_ref, shift_ref = take(8)
    dense, acc, first, hidden, before = take(5)
    total_split = take(parts)
    hosted = take(parts)
    replica = take(parts)
    f_in = [take(parts) for _ in range(2)]
    f_out = [take(parts) for _ in range(2)]
    p_in = [take(parts) for _ in range(2)]
    p_out = [take(parts) for _ in range(2)]
    z_out, z_in, xy_out, xy_in = take(4)
    local_sem, f_send, f_recv, p_send, p_recv, z_send, z_recv, xy_send, xy_recv = take(9)

    gx, gy, gz = lax.axis_index("gx"), lax.axis_index("gy"), lax.axis_index("gz")
    loads = [
        pltpu.make_async_copy(src, dst, local_sem.at[i])
        for i, (src, dst) in enumerate(
            zip(
                (
                    root_hbm,
                    block_hbm,
                    features_hbm,
                    columns_hbm,
                    present_hbm,
                    tiles_hbm,
                    self_one_hbm,
                    neigh_one_hbm,
                    self_two_hbm,
                    neigh_two_hbm,
                    scale_hbm,
                    shift_hbm,
                ),
                (
                    root_ref,
                    block_ref,
                    feat,
                    columns_ref,
                    present_ref,
                    tiles,
                    ws1,
                    wn1,
                    ws2,
                    wn2,
                    scale_ref,
                    shift_ref,
                ),
            )
        )
    ]
    for load in loads:
        load.start()

    def ahead(j):
        return lax.rem(gz + j, group)

    def behind(j):
        return lax.rem(gz + group - j, group)

    spots = [(i, k) for i in range(nx) for k in range(ny) if (i, k) != (0, 0)]

    def spot_id(spot):
        return {"gx": lax.rem(gx + spot[0], nx), "gy": lax.rem(gy + spot[1], ny)}

    barrier = pltpu.get_barrier_semaphore()
    for j in range(1, group):
        pl.semaphore_signal(
            barrier, inc=1, device_id={"gz": ahead(j)}, device_id_type=pl.DeviceIdType.MESH
        )
    for spot in spots:
        pl.semaphore_signal(
            barrier, inc=1, device_id=spot_id(spot), device_id_type=pl.DeviceIdType.MESH
        )

    def z_copy(src, dst, send, recv, j):
        return pltpu.make_async_remote_copy(
            src_ref=src,
            dst_ref=dst,
            send_sem=send,
            recv_sem=recv,
            device_id={"gz": ahead(j)},
            device_id_type=pl.DeviceIdType.MESH,
        )

    def f_copy(l, c, j):
        return z_copy(
            f_out[l][c].at[j - 1], f_in[l][c].at[j - 1], f_send.at[l, c, j - 1], f_recv.at[l, c, j - 1], j
        )

    def p_copy(l, c, j):
        return z_copy(
            p_out[l][c].at[j - 1], p_in[l][c].at[j - 1], p_send.at[l, c, j - 1], p_recv.at[l, c, j - 1], j
        )

    def zs_copy(j):
        return z_copy(z_out, z_in.at[j - 1], z_send.at[j - 1], z_recv.at[j - 1], j)

    def xy_copy(n):
        return pltpu.make_async_remote_copy(
            src_ref=xy_out,
            dst_ref=xy_in.at[n],
            send_sem=xy_send.at[n],
            recv_sem=xy_recv.at[n],
            device_id=spot_id(spots[n]),
            device_id_type=pl.DeviceIdType.MESH,
        )

    def lanes(c):
        return slice(c * LANES, (c + 1) * LANES)

    def wanted(j):
        q = ahead(j)
        sel = jnp.int32(0)
        for h in range(hosts):
            at = q * hosts + h
            sel = jnp.where(root_ref[at] == gz, block_ref[at], sel)
        return sel

    def spread(l, c, block):
        for j in range(1, group):
            f_out[l][c][j - 1] = block(wanted(j))
            f_copy(l, c, j).start()

    for load in loads[:3]:
        load.wait()
    pl.semaphore_wait(barrier, peers + len(spots))
    for c in range(parts):
        spread(0, c, lambda sel: feat[OWN + sel][:, lanes(c)])

    for load in loads[3:6]:
        load.wait()

    def build(b, carry):
        at = pl.multiple_of(b * tile, tile)
        for c in range(slots):
            total = jnp.zeros((tile, tile), BF16)
            for k in range(ks):
                on = (columns_ref[b, k] == c) & (present_ref[b, k] > 0)
                total = total + jnp.where(on, tiles[b, k], jnp.zeros((tile, tile), BF16))
            dense[pl.ds(at, tile), c * tile : (c + 1) * tile] = total
        return carry

    lax.fori_loop(0, slots, build, 0)
    for load in loads[6:]:
        load.wait()

    def blocks_of(n):
        return 2 * tile if n % (2 * tile) == 0 else tile

    def local(rows, start, stop):
        step = blocks_of(stop - start)
        flat = rows.reshape(rows_n, width)

        def one(i, carry):
            at = pl.multiple_of(start + i * step, tile)
            acc[pl.ds(at, step), :] = dot(dense[pl.ds(at, step), 0:rows_n], flat[...])
            return carry

        lax.fori_loop(0, (stop - start) // step, one, 0)

    def arrived(l, c):
        for j in range(1, group):
            f_copy(l, c, j).wait_recv()

    def unpack(l, c):
        blocks = []
        for h in range(hosts):
            root = root_ref[gz * hosts + h]
            at = jnp.maximum(lax.rem(gz - root + group, group) - 1, 0)
            blocks.append(f_in[l][c][at])
        return jnp.concatenate(blocks, axis=0)

    def collect(l, c):
        part = acc[rows_n:, lanes(c)] + dot(dense[rows_n:, rows_n:], hosted[c][...])
        replica[c][...] = part.astype(BF16).reshape(hosts, tile, LANES)
        for j in range(1, group):
            target = ahead(j)
            sel = jnp.int32(0)
            for h in range(hosts):
                sel = jnp.where(root_ref[gz * hosts + h] == target, h, sel)
            p_out[l][c][j - 1] = replica[c][sel]
            p_copy(l, c, j).start()

    split_n = rows_n - own_n

    def with_hosted(at, n):
        return [
            acc[pl.ds(at, n), lanes(c)] + dot(dense[pl.ds(at, n), rows_n:], hosted[c][...])
            for c in range(parts)
        ]

    def own(rows, w_self, w_neigh, emit):
        flat = rows.reshape(rows_n, width)
        step = blocks_of(own_n)

        def one(i, carry):
            at = pl.multiple_of(i * step, step)
            neighbours = jnp.concatenate(with_hosted(at, step), axis=1).astype(BF16)
            emit(
                pl.ds(at, step),
                dot(flat[pl.ds(at, step), :], w_self[...]) + dot(neighbours, w_neigh[...]),
            )
            return carry

        lax.fori_loop(0, own_n // step, one, 0)
        for c, value in enumerate(with_hosted(own_n, split_n)):
            acc[own_n:rows_n, lanes(c)] = value
        return dot(flat[own_n:rows_n, :], w_self[...])

    def receive(l, c):
        for j in range(1, group):
            p_copy(l, c, j).wait_recv()
        for s in range(SPLIT):
            at = own_n + s * tile
            total = acc[at : at + tile, lanes(c)]
            for j in range(1, group):
                q = behind(j)
                count = jnp.int32(0)
                for h in range(hosts):
                    spot = q * hosts + h
                    count = count + jnp.where((root_ref[spot] == gz) & (block_ref[spot] == s), 1, 0)
                total = total + count.astype(F32) * p_in[l][c][j - 1].astype(F32)
            total_split[c][s] = total.astype(BF16)

    def split_neighbours():
        return jnp.concatenate(
            [total_split[c][...].reshape(split_n, LANES) for c in range(parts)], axis=1
        )

    local(feat, rows_n, slots * tile)
    local(feat, 0, rows_n)
    for c in range(parts):
        arrived(0, c)
        hosted[c][...] = unpack(0, c)
        collect(0, c)

    def keep(at, value):
        first[at, :] = value

    selfs = own(feat, ws1, wn1, keep)
    before[...] = dot(jnp.concatenate([hosted[c][...] for c in range(parts)], axis=1), ws1[...])
    value = first[0:own_n, :]
    sums = jnp.sum(value, axis=0, keepdims=True)
    squares = jnp.sum(value * value, axis=0, keepdims=True)

    for c in range(parts):
        receive(0, c)
        spread(1, c, lambda sel: total_split[c][sel])
    value = selfs + dot(split_neighbours(), wn1[...])
    first[own_n:rows_n, :] = value
    sums = sums + jnp.sum(value, axis=0, keepdims=True)
    squares = squares + jnp.sum(value * value, axis=0, keepdims=True)

    total = jnp.concatenate([sums, squares, jnp.zeros((6, width), F32)], axis=0)
    xy_out[...] = total
    for n in range(len(spots)):
        xy_copy(n).start()
    for n in range(len(spots)):
        xy_copy(n).wait_recv()
        total = total + xy_in[n]
    z_out[...] = total
    for j in range(1, group):
        zs_copy(j).start()
    for j in range(1, group):
        zs_copy(j).wait_recv()
        total = total + z_in[j - 1]
    count = rows_n * nx * ny * group
    mean = total[0:1, :] / count
    var = total[1:2, :] / count - mean * mean
    gain = lax.rsqrt(var + 1e-05) * scale_ref[...]
    shift = shift_ref[...]

    def normal(value):
        return jnp.maximum((value - mean) * gain + shift, 0.0).astype(BF16)

    hidden[...] = normal(first[...]).reshape(rooted, tile, width)
    local(hidden, rows_n, slots * tile)
    for c in range(parts):
        arrived(1, c)
    totals = jnp.concatenate([unpack(1, c) for c in range(parts)], axis=1)
    view = normal(before[...] + dot(totals, wn1[...]))
    for c in range(parts):
        hosted[c][...] = view[:, lanes(c)]
        collect(1, c)

    def finish(at, value):
        out_ref[at, :] = value.astype(BF16)

    local(hidden, 0, rows_n)
    selfs = own(hidden, ws2, wn2, finish)
    for c in range(parts):
        receive(1, c)
    finish(slice(own_n, rows_n), selfs + dot(split_neighbours(), wn2[...]))

    for l in range(2):
        for c in range(parts):
            for j in range(1, group):
                f_copy(l, c, j).wait_send()
                p_copy(l, c, j).wait_send()
    for j in range(1, group):
        zs_copy(j).wait_send()
    for n in range(len(spots)):
        xy_copy(n).wait_send()


def per_device(
    features,
    tile_values,
    tile_columns,
    tile_present,
    host_root,
    host_block,
    self_one,
    neigh_one,
    scale_one,
    shift_one,
    self_two,
    neigh_two,
):
    slots, ks, tile, _ = tile_values.shape
    width = features.shape[1]
    rooted = features.shape[0] // tile
    hosts = slots - rooted
    nx, ny, group = (lax.axis_size(name) for name in ("gx", "gy", "gz"))
    peers, spots = group - 1, nx * ny - 1
    parts = width // LANES
    rows_n = rooted * tile
    sizes = (nx, ny, group, slots, ks, tile, width, rooted)

    box = pltpu.VMEM((peers, tile, LANES), BF16)
    dma = pltpu.SemaphoreType.DMA
    scratch = [
        *[pltpu.SMEM(tile_columns.shape, jnp.int32)] * 2,
        *[pltpu.SMEM(host_root.shape, jnp.int32)] * 2,
        pltpu.VMEM((rooted, tile, width), BF16),
        pltpu.VMEM(tile_values.shape, BF16),
        *[pltpu.VMEM((width, width), BF16)] * 4,
        *[pltpu.VMEM((1, width), F32)] * 2,
        pltpu.VMEM((slots * tile, slots * tile), BF16),
        pltpu.VMEM((slots * tile, width), F32),
        pltpu.VMEM((rows_n, width), F32),
        pltpu.VMEM((rooted, tile, width), BF16),
        pltpu.VMEM((hosts * tile, width), F32),
        *[pltpu.VMEM((SPLIT, tile, LANES), BF16)] * parts,
        *[pltpu.VMEM((hosts * tile, LANES), BF16)] * parts,
        *[pltpu.VMEM((hosts, tile, LANES), BF16)] * parts,
        *[box] * (8 * parts),
        pltpu.VMEM((8, width), F32),
        pltpu.VMEM((peers, 8, width), F32),
        pltpu.VMEM((8, width), F32),
        pltpu.VMEM((spots, 8, width), F32),
        dma((12,)),
        *[dma((2, parts, peers))] * 4,
        *[dma((peers,))] * 2,
        *[dma((spots,))] * 2,
    ]
    vmem = pl.BlockSpec(memory_space=pltpu.VMEM)
    hbm = pl.BlockSpec(memory_space=pltpu.HBM)
    call = pl.pallas_call(
        functools.partial(kernel, sizes),
        out_shape=jax.ShapeDtypeStruct((rows_n, width), BF16),
        in_specs=[hbm] * 12,
        out_specs=vmem,
        scratch_shapes=scratch,
        compiler_params=pltpu.CompilerParams(
            collective_id=0, has_side_effects=True, vmem_limit_bytes=40 * 1024 * 1024
        ),
    )
    operands = (
        tile_columns,
        tile_present,
        host_root,
        host_block,
        features.reshape(rooted, tile, width),
        tile_values,
        self_one,
        neigh_one,
        self_two,
        neigh_two,
        scale_one.reshape(1, width),
        shift_one.reshape(1, width),
    )
    return call(*(pltpu.with_memory_space_constraint(x, pltpu.HBM) for x in operands))


def solution(mesh):
    return jax.shard_map(
        per_device,
        mesh=mesh,
        in_specs=(
            P(("gx", "gy", "gz"), None),
            P(("gx", "gy", "gz"), None, None, None),
            P(("gx", "gy", "gz"), None),
            P(("gx", "gy", "gz"), None),
            P(("gx", "gy")),
            P(("gx", "gy")),
            P(),
            P(),
            P(),
            P(),
            P(),
            P(),
        ),
        out_specs=P(("gx", "gy", "gz"), None),
        check_vma=False,
    )
```

```python
import functools

import jax
import jax.numpy as jnp
from jax import lax
from jax.experimental import pallas as pl
from jax.experimental.pallas import tpu as pltpu
from jax.sharding import PartitionSpec as P

OWN = 4
SPLIT = 2
LANES = 128
F32 = jnp.float32
BF16 = jnp.bfloat16


def dot(a, b):
    return jnp.dot(a, b, preferred_element_type=F32)


def kernel(
    sizes,
    columns_hbm,
    present_hbm,
    root_hbm,
    block_hbm,
    features_hbm,
    tiles_hbm,
    self_one_hbm,
    neigh_one_hbm,
    self_two_hbm,
    neigh_two_hbm,
    scale_hbm,
    shift_hbm,
    out_ref,
    *scratch,
):
    nx, ny, group, slots, ks, tile, width, rooted = sizes
    hosts = slots - rooted
    rows_n = rooted * tile
    own_n = OWN * tile
    parts = width // LANES
    peers = group - 1
    scratch = list(scratch)

    def take(n):
        got = scratch[:n]
        del scratch[:n]
        return got

    columns_ref, present_ref, root_ref, block_ref = take(4)
    feat, tiles, ws1, wn1, ws2, wn2, scale_ref, shift_ref = take(8)
    dense, acc, first, hidden, before = take(5)
    total_split = take(parts)
    hosted = take(parts)
    replica = take(parts)
    f_in = [take(parts) for _ in range(2)]
    f_out = [take(parts) for _ in range(2)]
    p_in = [take(parts) for _ in range(2)]
    p_out = [take(parts) for _ in range(2)]
    z_out, z_in, xy_out, xy_in = take(4)
    local_sem, f_send, f_recv, p_send, p_recv, z_send, z_recv, xy_send, xy_recv = take(9)

    gx, gy, gz = lax.axis_index("gx"), lax.axis_index("gy"), lax.axis_index("gz")
    sources = (
        (root_hbm, root_ref),
        (block_hbm, block_ref),
        (features_hbm.at[OWN:], feat.at[OWN:]),
        (columns_hbm, columns_ref),
        (present_hbm, present_ref),
        (features_hbm.at[:OWN], feat.at[:OWN]),
        (tiles_hbm.at[OWN:], tiles.at[OWN:]),
        (tiles_hbm.at[:OWN], tiles.at[:OWN]),
        (self_one_hbm, ws1),
        (neigh_one_hbm, wn1),
        (self_two_hbm, ws2),
        (neigh_two_hbm, wn2),
        (scale_hbm, scale_ref),
        (shift_hbm, shift_ref),
    )
    loads = [
        pltpu.make_async_copy(src, dst, local_sem.at[i]) for i, (src, dst) in enumerate(sources)
    ]

    def ahead(j):
        return lax.rem(gz + j, group)

    def behind(j):
        return lax.rem(gz + group - j, group)

    spots = [(i, k) for i in range(nx) for k in range(ny) if (i, k) != (0, 0)]

    def spot_id(spot):
        return {"gx": lax.rem(gx + spot[0], nx), "gy": lax.rem(gy + spot[1], ny)}

    barrier = pltpu.get_barrier_semaphore()
    for j in range(1, group):
        pl.semaphore_signal(
            barrier, inc=1, device_id={"gz": ahead(j)}, device_id_type=pl.DeviceIdType.MESH
        )
    for spot in spots:
        pl.semaphore_signal(
            barrier, inc=1, device_id=spot_id(spot), device_id_type=pl.DeviceIdType.MESH
        )

    for load in loads:
        load.start()

    def z_copy(src, dst, send, recv, j):
        return pltpu.make_async_remote_copy(
            src_ref=src,
            dst_ref=dst,
            send_sem=send,
            recv_sem=recv,
            device_id={"gz": ahead(j)},
            device_id_type=pl.DeviceIdType.MESH,
        )

    def f_copy(l, c, j):
        return z_copy(
            f_out[l][c].at[j - 1], f_in[l][c].at[j - 1], f_send.at[l, c, j - 1], f_recv.at[l, c, j - 1], j
        )

    def p_copy(l, c, j):
        return z_copy(
            p_out[l][c].at[j - 1], p_in[l][c].at[j - 1], p_send.at[l, c, j - 1], p_recv.at[l, c, j - 1], j
        )

    def zs_copy(j):
        return z_copy(z_out, z_in.at[j - 1], z_send.at[j - 1], z_recv.at[j - 1], j)

    def xy_copy(n):
        return pltpu.make_async_remote_copy(
            src_ref=xy_out,
            dst_ref=xy_in.at[n],
            send_sem=xy_send.at[n],
            recv_sem=xy_recv.at[n],
            device_id=spot_id(spots[n]),
            device_id_type=pl.DeviceIdType.MESH,
        )

    def lanes(c):
        return slice(c * LANES, (c + 1) * LANES)

    def wanted(j):
        q = ahead(j)
        sel = jnp.int32(0)
        for h in range(hosts):
            at = q * hosts + h
            sel = jnp.where(root_ref[at] == gz, block_ref[at], sel)
        return sel

    def spread(l, c, block):
        for j in range(1, group):
            f_out[l][c][j - 1] = block(wanted(j))
            f_copy(l, c, j).start()

    def split_feature(sel, c):
        block = feat[OWN, :, lanes(c)]
        for s in range(1, SPLIT):
            block = jnp.where(sel == s, feat[OWN + s, :, lanes(c)], block)
        return block

    for load in loads[:3]:
        load.wait()
    pl.semaphore_wait(barrier, peers + len(spots))
    for c in range(parts):
        spread(0, c, lambda sel: split_feature(sel, c))

    for load in loads[3:7]:
        load.wait()

    def build(b, carry):
        at = pl.multiple_of(b * tile, tile)
        for c in range(slots):
            total = jnp.zeros((tile, tile), BF16)
            for k in range(ks):
                on = (columns_ref[b, k] == c) & (present_ref[b, k] > 0)
                total = total + jnp.where(on, tiles[b, k], jnp.zeros((tile, tile), BF16))
            dense[pl.ds(at, tile), c * tile : (c + 1) * tile] = total
        return carry

    def blocks_of(n):
        return 2 * tile if n % (2 * tile) == 0 else tile

    def local(rows, start, stop):
        step = blocks_of(stop - start)
        flat = rows.reshape(rows_n, width)

        def one(i, carry):
            at = pl.multiple_of(start + i * step, tile)
            acc[pl.ds(at, step), :] = dot(dense[pl.ds(at, step), 0:rows_n], flat[...])
            return carry

        lax.fori_loop(0, (stop - start) // step, one, 0)

    def arrived(l, c):
        for j in range(1, group):
            f_copy(l, c, j).wait_recv()

    def unpack(l, c):
        blocks = []
        for h in range(hosts):
            root = root_ref[gz * hosts + h]
            at = jnp.maximum(lax.rem(gz - root + group, group) - 1, 0)
            blocks.append(f_in[l][c][at])
        return jnp.concatenate(blocks, axis=0)

    def collect(l, c):
        part = acc[rows_n:, lanes(c)] + dot(dense[rows_n:, rows_n:], hosted[c][...])
        replica[c][...] = part.astype(BF16).reshape(hosts, tile, LANES)
        for j in range(1, group):
            target = ahead(j)
            sel = jnp.int32(0)
            for h in range(hosts):
                sel = jnp.where(root_ref[gz * hosts + h] == target, h, sel)
            p_out[l][c][j - 1] = replica[c][sel]
            p_copy(l, c, j).start()

    split_n = rows_n - own_n

    def with_hosted(at, n):
        return [
            acc[pl.ds(at, n), lanes(c)] + dot(dense[pl.ds(at, n), rows_n:], hosted[c][...])
            for c in range(parts)
        ]

    def split_hosted():
        for c, value in enumerate(with_hosted(own_n, split_n)):
            acc[own_n:rows_n, lanes(c)] = value

    def own(rows, w_self, w_neigh, start, stop, emit):
        flat = rows.reshape(rows_n, width)
        step = blocks_of(stop - start)

        def one(i, carry):
            at = pl.multiple_of(start + i * step, tile)
            neighbours = jnp.concatenate(with_hosted(at, step), axis=1).astype(BF16)
            emit(
                pl.ds(at, step),
                dot(flat[pl.ds(at, step), :], w_self[...]) + dot(neighbours, w_neigh[...]),
            )
            return carry

        lax.fori_loop(0, (stop - start) // step, one, 0)

    def split_self(rows, w_self):
        return dot(rows.reshape(rows_n, width)[own_n:rows_n, :], w_self[...])

    def split_neigh(c, w_neigh):
        return dot(total_split[c][...].reshape(split_n, LANES), w_neigh[lanes(c), :])

    def receive(l, c):
        for j in range(1, group):
            p_copy(l, c, j).wait_recv()
        for s in range(SPLIT):
            at = own_n + s * tile
            total = acc[at : at + tile, lanes(c)]
            for j in range(1, group):
                q = behind(j)
                count = jnp.int32(0)
                for h in range(hosts):
                    spot = q * hosts + h
                    count = count + jnp.where((root_ref[spot] == gz) & (block_ref[spot] == s), 1, 0)
                total = total + count.astype(F32) * p_in[l][c][j - 1].astype(F32)
            total_split[c][s] = total.astype(BF16)

    lax.fori_loop(rooted, slots, build, 0)
    local(feat, rows_n, slots * tile)
    lax.fori_loop(OWN, rooted, build, 0)
    local(feat, own_n, rows_n)
    for c in range(parts):
        arrived(0, c)
        hosted[c][...] = unpack(0, c)
        collect(0, c)
    split_hosted()
    for load in loads[7:]:
        load.wait()

    def keep(at, value):
        first[at, :] = value

    edges = [own_n * i // parts // tile * tile for i in range(parts + 1)]
    value = split_self(feat, ws1)
    for c in range(parts):
        start, stop = edges[c], edges[c + 1]
        lax.fori_loop(start // tile, stop // tile, build, 0)
        local(feat, start, stop)
        own(feat, ws1, wn1, start, stop, keep)
        if c == parts - 1:
            mine = first[0:own_n, :]
            sums = jnp.sum(mine, axis=0, keepdims=True)
            squares = jnp.sum(mine * mine, axis=0, keepdims=True)
        receive(0, c)
        if c < parts - 1:
            spread(1, c, lambda sel: total_split[c][sel])
        value = value + split_neigh(c, wn1)
    first[own_n:rows_n, :] = value
    sums = sums + jnp.sum(value, axis=0, keepdims=True)
    squares = squares + jnp.sum(value * value, axis=0, keepdims=True)

    total = jnp.concatenate([sums, squares, jnp.zeros((6, width), F32)], axis=0)
    z_out[...] = total
    for j in range(1, group):
        zs_copy(j).start()
    spread(1, parts - 1, lambda sel: total_split[parts - 1][sel])
    before[...] = dot(jnp.concatenate([hosted[c][...] for c in range(parts)], axis=1), ws1[...])
    for j in range(1, group):
        zs_copy(j).wait_recv()
        total = total + z_in[j - 1]
    xy_out[...] = total
    for n in range(len(spots)):
        xy_copy(n).start()
    for c in range(parts - 1):
        arrived(1, c)
        before[...] += dot(unpack(1, c), wn1[lanes(c), :])
    for n in range(len(spots)):
        xy_copy(n).wait_recv()
        total = total + xy_in[n]
    count = rows_n * nx * ny * group
    mean = total[0:1, :] / count
    var = total[1:2, :] / count - mean * mean
    gain = lax.rsqrt(var + 1e-05) * scale_ref[...]
    shift = shift_ref[...]

    def normal(value):
        return jnp.maximum((value - mean) * gain + shift, 0.0).astype(BF16)

    hidden[...] = normal(first[...]).reshape(rooted, tile, width)
    local(hidden, rows_n, slots * tile)
    arrived(1, parts - 1)
    view = normal(before[...] + dot(unpack(1, parts - 1), wn1[lanes(parts - 1), :]))
    for c in range(parts):
        hosted[c][...] = view[:, lanes(c)]
        collect(1, c)

    def finish(at, value):
        out_ref[at, :] = value.astype(BF16)

    local(hidden, own_n, rows_n)
    split_hosted()
    value = split_self(hidden, ws2)
    local(hidden, 0, own_n)
    own(hidden, ws2, wn2, 0, own_n, finish)
    for c in range(parts):
        receive(1, c)
        value = value + split_neigh(c, wn2)
    finish(slice(own_n, rows_n), value)

    for l in range(2):
        for c in range(parts):
            for j in range(1, group):
                f_copy(l, c, j).wait_send()
                p_copy(l, c, j).wait_send()
    for j in range(1, group):
        zs_copy(j).wait_send()
    for n in range(len(spots)):
        xy_copy(n).wait_send()


def per_device(
    features,
    tile_values,
    tile_columns,
    tile_present,
    host_root,
    host_block,
    self_one,
    neigh_one,
    scale_one,
    shift_one,
    self_two,
    neigh_two,
):
    slots, ks, tile, _ = tile_values.shape
    width = features.shape[1]
    rooted = features.shape[0] // tile
    hosts = slots - rooted
    nx, ny, group = (lax.axis_size(name) for name in ("gx", "gy", "gz"))
    peers, spots = group - 1, nx * ny - 1
    parts = width // LANES
    rows_n = rooted * tile
    sizes = (nx, ny, group, slots, ks, tile, width, rooted)

    box = pltpu.VMEM((peers, tile, LANES), BF16)
    dma = pltpu.SemaphoreType.DMA
    scratch = [
        *[pltpu.SMEM(tile_columns.shape, jnp.int32)] * 2,
        *[pltpu.SMEM(host_root.shape, jnp.int32)] * 2,
        pltpu.VMEM((rooted, tile, width), BF16),
        pltpu.VMEM(tile_values.shape, BF16),
        *[pltpu.VMEM((width, width), BF16)] * 4,
        *[pltpu.VMEM((1, width), F32)] * 2,
        pltpu.VMEM((slots * tile, slots * tile), BF16),
        pltpu.VMEM((slots * tile, width), F32),
        pltpu.VMEM((rows_n, width), F32),
        pltpu.VMEM((rooted, tile, width), BF16),
        pltpu.VMEM((hosts * tile, width), F32),
        *[pltpu.VMEM((SPLIT, tile, LANES), BF16)] * parts,
        *[pltpu.VMEM((hosts * tile, LANES), BF16)] * parts,
        *[pltpu.VMEM((hosts, tile, LANES), BF16)] * parts,
        *[box] * (8 * parts),
        pltpu.VMEM((8, width), F32),
        pltpu.VMEM((peers, 8, width), F32),
        pltpu.VMEM((8, width), F32),
        pltpu.VMEM((spots, 8, width), F32),
        dma((14,)),
        *[dma((2, parts, peers))] * 4,
        *[dma((peers,))] * 2,
        *[dma((spots,))] * 2,
    ]
    vmem = pl.BlockSpec(memory_space=pltpu.VMEM)
    hbm = pl.BlockSpec(memory_space=pltpu.HBM)
    call = pl.pallas_call(
        functools.partial(kernel, sizes),
        out_shape=jax.ShapeDtypeStruct((rows_n, width), BF16),
        in_specs=[hbm] * 12,
        out_specs=vmem,
        scratch_shapes=scratch,
        compiler_params=pltpu.CompilerParams(
            collective_id=0, has_side_effects=True, vmem_limit_bytes=40 * 1024 * 1024
        ),
    )
    operands = (
        tile_columns,
        tile_present,
        host_root,
        host_block,
        features.reshape(rooted, tile, width),
        tile_values,
        self_one,
        neigh_one,
        self_two,
        neigh_two,
        scale_one.reshape(1, width),
        shift_one.reshape(1, width),
    )
    return call(*(pltpu.with_memory_space_constraint(x, pltpu.HBM) for x in operands))


def solution(mesh):
    return jax.shard_map(
        per_device,
        mesh=mesh,
        in_specs=(
            P(("gx", "gy", "gz"), None),
            P(("gx", "gy", "gz"), None, None, None),
            P(("gx", "gy", "gz"), None),
            P(("gx", "gy", "gz"), None),
            P(("gx", "gy")),
            P(("gx", "gy")),
            P(),
            P(),
            P(),
            P(),
            P(),
            P(),
        ),
        out_specs=P(("gx", "gy", "gz"), None),
        check_vma=False,
    )
```

```python
import functools

import jax
import jax.numpy as jnp
from jax import lax
from jax.experimental import pallas as pl
from jax.experimental.pallas import tpu as pltpu
from jax.sharding import PartitionSpec as P

OWN = 4
SPLIT = 2
LANES = 128
F32 = jnp.float32
BF16 = jnp.bfloat16


def dot(a, b):
    return jnp.dot(a, b, preferred_element_type=F32)


def kernel(
    sizes,
    columns_hbm,
    present_hbm,
    root_hbm,
    block_hbm,
    features_hbm,
    tiles_hbm,
    self_one_hbm,
    neigh_one_hbm,
    self_two_hbm,
    neigh_two_hbm,
    scale_hbm,
    shift_hbm,
    out_ref,
    *scratch,
):
    nx, ny, group, slots, ks, tile, width, rooted = sizes
    hosts = slots - rooted
    rows_n = rooted * tile
    own_n = OWN * tile
    parts = width // LANES
    peers = group - 1
    scratch = list(scratch)

    def take(n):
        got = scratch[:n]
        del scratch[:n]
        return got

    columns_ref, present_ref, root_ref, block_ref = take(4)
    feat, tiles, ws1, wn1, ws2, wn2, scale_ref, shift_ref = take(8)
    dense, acc, first, hidden, before = take(5)
    total_split = take(parts)
    hosted = take(parts)
    replica = take(parts)
    f_in = [take(parts) for _ in range(2)]
    f_out = [take(parts) for _ in range(2)]
    p_in = [take(parts) for _ in range(2)]
    p_out = [take(parts) for _ in range(2)]
    z_out, z_in, xy_out, xy_in = take(4)
    local_sem, f_send, f_recv, p_send, p_recv, z_send, z_recv, xy_send, xy_recv = take(9)

    gx, gy, gz = lax.axis_index("gx"), lax.axis_index("gy"), lax.axis_index("gz")
    sources = (
        (root_hbm, root_ref),
        (block_hbm, block_ref),
        (features_hbm.at[OWN:], feat.at[OWN:]),
        (columns_hbm, columns_ref),
        (present_hbm, present_ref),
        (tiles_hbm, tiles),
        (features_hbm.at[:OWN], feat.at[:OWN]),
        (self_one_hbm, ws1),
        (neigh_one_hbm, wn1),
        (self_two_hbm, ws2),
        (neigh_two_hbm, wn2),
        (scale_hbm, scale_ref),
        (shift_hbm, shift_ref),
    )
    loads = [
        pltpu.make_async_copy(src, dst, local_sem.at[i]) for i, (src, dst) in enumerate(sources)
    ]

    def ahead(j):
        return lax.rem(gz + j, group)

    def behind(j):
        return lax.rem(gz + group - j, group)

    spots = [(i, k) for i in range(nx) for k in range(ny) if (i, k) != (0, 0)]

    def spot_id(spot):
        return {"gx": lax.rem(gx + spot[0], nx), "gy": lax.rem(gy + spot[1], ny)}

    barrier = pltpu.get_barrier_semaphore()
    for j in range(1, group):
        pl.semaphore_signal(
            barrier, inc=1, device_id={"gz": ahead(j)}, device_id_type=pl.DeviceIdType.MESH
        )
    for spot in spots:
        pl.semaphore_signal(
            barrier, inc=1, device_id=spot_id(spot), device_id_type=pl.DeviceIdType.MESH
        )

    for load in loads:
        load.start()

    def z_copy(src, dst, send, recv, j):
        return pltpu.make_async_remote_copy(
            src_ref=src,
            dst_ref=dst,
            send_sem=send,
            recv_sem=recv,
            device_id={"gz": ahead(j)},
            device_id_type=pl.DeviceIdType.MESH,
        )

    def f_copy(l, c, j):
        return z_copy(
            f_out[l][c].at[j - 1], f_in[l][c].at[j - 1], f_send.at[l, c, j - 1], f_recv.at[l, c, j - 1], j
        )

    def p_copy(l, c, j):
        return z_copy(
            p_out[l][c].at[j - 1], p_in[l][c].at[j - 1], p_send.at[l, c, j - 1], p_recv.at[l, c, j - 1], j
        )

    def zs_copy(j):
        return z_copy(z_out, z_in.at[j - 1], z_send.at[j - 1], z_recv.at[j - 1], j)

    def xy_copy(n):
        return pltpu.make_async_remote_copy(
            src_ref=xy_out,
            dst_ref=xy_in.at[n],
            send_sem=xy_send.at[n],
            recv_sem=xy_recv.at[n],
            device_id=spot_id(spots[n]),
            device_id_type=pl.DeviceIdType.MESH,
        )

    def lanes(c):
        return slice(c * LANES, (c + 1) * LANES)

    def wanted(j):
        q = ahead(j)
        sel = jnp.int32(0)
        for h in range(hosts):
            at = q * hosts + h
            sel = jnp.where(root_ref[at] == gz, block_ref[at], sel)
        return sel

    def order(k):
        return jnp.where(2 * gz < group, group - k, k)

    def spread(l, c, block, start=1, stop=group):
        for k in range(start, stop):
            j = order(k)
            f_out[l][c][j - 1] = block(wanted(j))
            f_copy(l, c, j).start()

    def split_feature(sel, c):
        block = feat[OWN, :, lanes(c)]
        for s in range(1, SPLIT):
            block = jnp.where(sel == s, feat[OWN + s, :, lanes(c)], block)
        return block

    for load in loads[:3]:
        load.wait()
    pl.semaphore_wait(barrier, peers + len(spots))
    for c in range(parts):
        spread(0, c, lambda sel: split_feature(sel, c))

    for load in loads[3:6]:
        load.wait()

    def build(b, carry):
        at = pl.multiple_of(b * tile, tile)
        for c in range(slots):
            total = jnp.zeros((tile, tile), BF16)
            for k in range(ks):
                on = (columns_ref[b, k] == c) & (present_ref[b, k] > 0)
                total = total + jnp.where(on, tiles[b, k], jnp.zeros((tile, tile), BF16))
            dense[pl.ds(at, tile), c * tile : (c + 1) * tile] = total
        return carry

    lax.fori_loop(0, slots, build, 0)
    for load in loads[6:]:
        load.wait()

    def blocks_of(n):
        return 2 * tile if n % (2 * tile) == 0 else tile

    def local(rows, start, stop):
        step = blocks_of(stop - start)
        flat = rows.reshape(rows_n, width)

        def one(i, carry):
            at = pl.multiple_of(start + i * step, tile)
            acc[pl.ds(at, step), :] = dot(dense[pl.ds(at, step), 0:rows_n], flat[...])
            return carry

        lax.fori_loop(0, (stop - start) // step, one, 0)

    def arrived(l, c):
        for j in range(1, group):
            f_copy(l, c, j).wait_recv()

    def unpack(l, c):
        blocks = []
        for h in range(hosts):
            root = root_ref[gz * hosts + h]
            at = jnp.maximum(lax.rem(gz - root + group, group) - 1, 0)
            blocks.append(f_in[l][c][at])
        return jnp.concatenate(blocks, axis=0)

    def collect(l, c):
        part = acc[rows_n:, lanes(c)] + dot(dense[rows_n:, rows_n:], hosted[c][...])
        replica[c][...] = part.astype(BF16).reshape(hosts, tile, LANES)
        for k in range(1, group):
            j = order(k)
            target = ahead(j)
            sel = jnp.int32(0)
            for h in range(hosts):
                sel = jnp.where(root_ref[gz * hosts + h] == target, h, sel)
            p_out[l][c][j - 1] = replica[c][sel]
            p_copy(l, c, j).start()

    split_n = rows_n - own_n

    def with_hosted(at, n):
        return [
            acc[pl.ds(at, n), lanes(c)] + dot(dense[pl.ds(at, n), rows_n:], hosted[c][...])
            for c in range(parts)
        ]

    def own(rows, w_self, w_neigh, emit):
        flat = rows.reshape(rows_n, width)
        step = blocks_of(own_n)

        def one(i, carry):
            at = pl.multiple_of(i * step, step)
            neighbours = jnp.concatenate(with_hosted(at, step), axis=1).astype(BF16)
            emit(
                pl.ds(at, step),
                dot(flat[pl.ds(at, step), :], w_self[...]) + dot(neighbours, w_neigh[...]),
            )
            return carry

        lax.fori_loop(0, own_n // step, one, 0)
        for c, value in enumerate(with_hosted(own_n, split_n)):
            acc[own_n:rows_n, lanes(c)] = value
        return dot(flat[own_n:rows_n, :], w_self[...])

    def receive(l, c):
        for j in range(1, group):
            p_copy(l, c, j).wait_recv()
        for s in range(SPLIT):
            at = own_n + s * tile
            total = acc[at : at + tile, lanes(c)]
            for j in range(1, group):
                q = behind(j)
                count = jnp.int32(0)
                for h in range(hosts):
                    spot = q * hosts + h
                    count = count + jnp.where((root_ref[spot] == gz) & (block_ref[spot] == s), 1, 0)
                total = total + count.astype(F32) * p_in[l][c][j - 1].astype(F32)
            total_split[c][s] = total.astype(BF16)

    def split_neigh(c, w_neigh):
        return dot(total_split[c][...].reshape(split_n, LANES), w_neigh[lanes(c), :])

    local(feat, rows_n, slots * tile)
    local(feat, 0, rows_n)
    for c in range(parts):
        arrived(0, c)
        hosted[c][...] = unpack(0, c)
        collect(0, c)

    def keep(at, value):
        first[at, :] = value

    value = own(feat, ws1, wn1, keep)
    before[...] = dot(jnp.concatenate([hosted[c][...] for c in range(parts)], axis=1), ws1[...])
    mine = first[0:own_n, :]
    sums = jnp.sum(mine, axis=0, keepdims=True)
    squares = jnp.sum(mine * mine, axis=0, keepdims=True)

    def totals_of(c):
        return lambda sel: total_split[c][sel]

    ahead_of_sums = 1 + peers // 3
    for c in range(parts):
        receive(0, c)
        value = value + split_neigh(c, wn1)
        if c == 0:
            spread(1, c, totals_of(c), 1, ahead_of_sums)
    first[own_n:rows_n, :] = value
    sums = sums + jnp.sum(value, axis=0, keepdims=True)
    squares = squares + jnp.sum(value * value, axis=0, keepdims=True)

    total = jnp.concatenate([sums, squares, jnp.zeros((6, width), F32)], axis=0)
    z_out[...] = total
    for j in range(1, group):
        zs_copy(j).start()
    spread(1, 0, totals_of(0), ahead_of_sums, group)
    for c in range(1, parts):
        spread(1, c, totals_of(c))
    for j in range(1, group):
        zs_copy(j).wait_recv()
        total = total + z_in[j - 1]
    xy_out[...] = total
    for n in range(len(spots)):
        xy_copy(n).start()
    for n in range(len(spots)):
        xy_copy(n).wait_recv()
        total = total + xy_in[n]
    count = rows_n * nx * ny * group
    mean = total[0:1, :] / count
    var = total[1:2, :] / count - mean * mean
    gain = lax.rsqrt(var + 1e-05) * scale_ref[...]
    shift = shift_ref[...]

    def normal(value):
        return jnp.maximum((value - mean) * gain + shift, 0.0).astype(BF16)

    hidden[...] = normal(first[...]).reshape(rooted, tile, width)
    local(hidden, rows_n, slots * tile)
    for c in range(parts - 1):
        arrived(1, c)
        before[...] += dot(unpack(1, c), wn1[lanes(c), :])
    arrived(1, parts - 1)
    view = normal(before[...] + dot(unpack(1, parts - 1), wn1[lanes(parts - 1), :]))
    for c in range(parts):
        hosted[c][...] = view[:, lanes(c)]
        collect(1, c)

    def finish(at, value):
        out_ref[at, :] = value.astype(BF16)

    local(hidden, 0, rows_n)
    value = own(hidden, ws2, wn2, finish)
    for c in range(parts):
        receive(1, c)
        value = value + split_neigh(c, wn2)
    finish(slice(own_n, rows_n), value)

    for l in range(2):
        for c in range(parts):
            for j in range(1, group):
                f_copy(l, c, j).wait_send()
                p_copy(l, c, j).wait_send()
    for j in range(1, group):
        zs_copy(j).wait_send()
    for n in range(len(spots)):
        xy_copy(n).wait_send()


def per_device(
    features,
    tile_values,
    tile_columns,
    tile_present,
    host_root,
    host_block,
    self_one,
    neigh_one,
    scale_one,
    shift_one,
    self_two,
    neigh_two,
):
    slots, ks, tile, _ = tile_values.shape
    width = features.shape[1]
    rooted = features.shape[0] // tile
    hosts = slots - rooted
    nx, ny, group = (lax.axis_size(name) for name in ("gx", "gy", "gz"))
    peers, spots = group - 1, nx * ny - 1
    parts = width // LANES
    rows_n = rooted * tile
    sizes = (nx, ny, group, slots, ks, tile, width, rooted)

    box = pltpu.VMEM((peers, tile, LANES), BF16)
    dma = pltpu.SemaphoreType.DMA
    scratch = [
        *[pltpu.SMEM(tile_columns.shape, jnp.int32)] * 2,
        *[pltpu.SMEM(host_root.shape, jnp.int32)] * 2,
        pltpu.VMEM((rooted, tile, width), BF16),
        pltpu.VMEM(tile_values.shape, BF16),
        *[pltpu.VMEM((width, width), BF16)] * 4,
        *[pltpu.VMEM((1, width), F32)] * 2,
        pltpu.VMEM((slots * tile, slots * tile), BF16),
        pltpu.VMEM((slots * tile, width), F32),
        pltpu.VMEM((rows_n, width), F32),
        pltpu.VMEM((rooted, tile, width), BF16),
        pltpu.VMEM((hosts * tile, width), F32),
        *[pltpu.VMEM((SPLIT, tile, LANES), BF16)] * parts,
        *[pltpu.VMEM((hosts * tile, LANES), BF16)] * parts,
        *[pltpu.VMEM((hosts, tile, LANES), BF16)] * parts,
        *[box] * (8 * parts),
        pltpu.VMEM((8, width), F32),
        pltpu.VMEM((peers, 8, width), F32),
        pltpu.VMEM((8, width), F32),
        pltpu.VMEM((spots, 8, width), F32),
        dma((13,)),
        *[dma((2, parts, peers))] * 4,
        *[dma((peers,))] * 2,
        *[dma((spots,))] * 2,
    ]
    vmem = pl.BlockSpec(memory_space=pltpu.VMEM)
    hbm = pl.BlockSpec(memory_space=pltpu.HBM)
    call = pl.pallas_call(
        functools.partial(kernel, sizes),
        out_shape=jax.ShapeDtypeStruct((rows_n, width), BF16),
        in_specs=[hbm] * 12,
        out_specs=vmem,
        scratch_shapes=scratch,
        compiler_params=pltpu.CompilerParams(
            collective_id=0, has_side_effects=True, vmem_limit_bytes=40 * 1024 * 1024
        ),
    )
    operands = (
        tile_columns,
        tile_present,
        host_root,
        host_block,
        features.reshape(rooted, tile, width),
        tile_values,
        self_one,
        neigh_one,
        self_two,
        neigh_two,
        scale_one.reshape(1, width),
        shift_one.reshape(1, width),
    )
    return call(*(pltpu.with_memory_space_constraint(x, pltpu.HBM) for x in operands))


def solution(mesh):
    return jax.shard_map(
        per_device,
        mesh=mesh,
        in_specs=(
            P(("gx", "gy", "gz"), None),
            P(("gx", "gy", "gz"), None, None, None),
            P(("gx", "gy", "gz"), None),
            P(("gx", "gy", "gz"), None),
            P(("gx", "gy")),
            P(("gx", "gy")),
            P(),
            P(),
            P(),
            P(),
            P(),
            P(),
        ),
        out_specs=P(("gx", "gy", "gz"), None),
        check_vma=False,
    )
```

```python
import functools

import jax
import jax.numpy as jnp
from jax import lax
from jax.experimental import pallas as pl
from jax.experimental.pallas import tpu as pltpu
from jax.sharding import PartitionSpec as P

OWN = 4
SPLIT = 2
LANES = 128
F32 = jnp.float32
BF16 = jnp.bfloat16


def dot(a, b):
    return jnp.dot(a, b, preferred_element_type=F32)


def kernel(
    sizes,
    columns_hbm,
    present_hbm,
    root_hbm,
    block_hbm,
    features_hbm,
    tiles_hbm,
    self_one_hbm,
    neigh_one_hbm,
    self_two_hbm,
    neigh_two_hbm,
    scale_hbm,
    shift_hbm,
    out_ref,
    *scratch,
):
    nx, ny, group, slots, ks, tile, width, rooted = sizes
    hosts = slots - rooted
    rows_n = rooted * tile
    own_n = OWN * tile
    parts = width // LANES
    peers = group - 1
    scratch = list(scratch)

    def take(n):
        got = scratch[:n]
        del scratch[:n]
        return got

    columns_ref, present_ref, root_ref, block_ref = take(4)
    feat, tiles, ws1, wn1, ws2, wn2, scale_ref, shift_ref = take(8)
    dense, acc, first, hidden, before = take(5)
    total_split = take(parts)
    hosted = take(parts)
    replica = take(parts)
    f_in = [take(parts) for _ in range(2)]
    f_out = [take(parts) for _ in range(2)]
    p_in = [take(parts) for _ in range(2)]
    p_out = [take(parts) for _ in range(2)]
    z_out, z_in, xy_out, xy_in = take(4)
    local_sem, f_send, f_recv, p_send, p_recv, z_send, z_recv, xy_send, xy_recv = take(9)

    gx, gy, gz = lax.axis_index("gx"), lax.axis_index("gy"), lax.axis_index("gz")
    sources = (
        (root_hbm, root_ref),
        (block_hbm, block_ref),
        (features_hbm.at[OWN:], feat.at[OWN:]),
        (columns_hbm, columns_ref),
        (present_hbm, present_ref),
        (tiles_hbm, tiles),
        (features_hbm.at[:OWN], feat.at[:OWN]),
        (self_one_hbm, ws1),
        (neigh_one_hbm, wn1),
        (self_two_hbm, ws2),
        (neigh_two_hbm, wn2),
        (scale_hbm, scale_ref),
        (shift_hbm, shift_ref),
    )
    loads = [
        pltpu.make_async_copy(src, dst, local_sem.at[i]) for i, (src, dst) in enumerate(sources)
    ]

    def wrap(value, size):
        return jnp.where(value >= size, value - size, value)

    def ahead(j):
        return wrap(gz + j, group)

    def behind(j):
        return wrap(gz + group - j, group)

    spots = [(i, k) for i in range(nx) for k in range(ny) if (i, k) != (0, 0)]

    def spot_id(spot):
        return {"gx": wrap(gx + spot[0], nx), "gy": wrap(gy + spot[1], ny)}

    barrier = pltpu.get_barrier_semaphore()
    for j in range(1, group):
        pl.semaphore_signal(
            barrier, inc=1, device_id={"gz": ahead(j)}, device_id_type=pl.DeviceIdType.MESH
        )
    for spot in spots:
        pl.semaphore_signal(
            barrier, inc=1, device_id=spot_id(spot), device_id_type=pl.DeviceIdType.MESH
        )

    for load in loads:
        load.start()

    def z_copy(src, dst, send, recv, j):
        return pltpu.make_async_remote_copy(
            src_ref=src,
            dst_ref=dst,
            send_sem=send,
            recv_sem=recv,
            device_id={"gz": ahead(j)},
            device_id_type=pl.DeviceIdType.MESH,
        )

    def f_copy(l, c, j):
        return z_copy(
            f_out[l][c].at[j - 1], f_in[l][c].at[j - 1], f_send.at[l, c, j - 1], f_recv.at[l, c, j - 1], j
        )

    def p_copy(l, c, j):
        return z_copy(
            p_out[l][c].at[j - 1], p_in[l][c].at[j - 1], p_send.at[l, c, j - 1], p_recv.at[l, c, j - 1], j
        )

    def zs_copy(j):
        return z_copy(z_out, z_in.at[j - 1], z_send.at[j - 1], z_recv.at[j - 1], j)

    def xy_copy(n):
        return pltpu.make_async_remote_copy(
            src_ref=xy_out,
            dst_ref=xy_in.at[n],
            send_sem=xy_send.at[n],
            recv_sem=xy_recv.at[n],
            device_id=spot_id(spots[n]),
            device_id_type=pl.DeviceIdType.MESH,
        )

    def lanes(c):
        return slice(c * LANES, (c + 1) * LANES)

    def wanted(j):
        q = ahead(j)
        sel = jnp.int32(0)
        for h in range(hosts):
            at = q * hosts + h
            sel = jnp.where(root_ref[at] == gz, block_ref[at], sel)
        return sel

    def spread(l, c, block):
        for j in range(1, group):
            f_out[l][c][j - 1] = block(wants[j])
            f_copy(l, c, j).start()

    def split_feature(sel, c):
        block = feat[OWN, :, lanes(c)]
        for s in range(1, SPLIT):
            block = jnp.where(sel == s, feat[OWN + s, :, lanes(c)], block)
        return block

    for load in loads[:2]:
        load.wait()
    wants = {j: wanted(j) for j in range(1, group)}
    my_roots = [root_ref[gz * hosts + h] for h in range(hosts)]
    from_at = []
    for root in my_roots:
        at = wrap(gz - root + group, group) - 1
        from_at.append(jnp.clip(at, 0, peers - 1))
    to_sel = {}
    holds = {}
    for j in range(1, group):
        target, q = ahead(j), behind(j)
        sel = jnp.int32(0)
        for h in range(hosts):
            sel = jnp.where(my_roots[h] == target, h, sel)
        to_sel[j] = sel
        for s in range(SPLIT):
            count = jnp.int32(0)
            for h in range(hosts):
                spot = q * hosts + h
                count = count + jnp.where((root_ref[spot] == gz) & (block_ref[spot] == s), 1, 0)
            holds[j, s] = count.astype(F32)
    loads[2].wait()
    pl.semaphore_wait(barrier, peers + len(spots))
    for c in range(parts):
        spread(0, c, lambda sel: split_feature(sel, c))

    for load in loads[3:6]:
        load.wait()

    def build(b, carry):
        at = pl.multiple_of(b * tile, tile)
        for c in range(slots):
            total = jnp.zeros((tile, tile), BF16)
            for k in range(ks):
                on = (columns_ref[b, k] == c) & (present_ref[b, k] > 0)
                total = total + jnp.where(on, tiles[b, k], jnp.zeros((tile, tile), BF16))
            dense[pl.ds(at, tile), c * tile : (c + 1) * tile] = total
        return carry

    lax.fori_loop(0, slots, build, 0)
    for load in loads[6:]:
        load.wait()

    def blocks_of(n):
        return 2 * tile if n % (2 * tile) == 0 else tile

    def local(rows, start, stop):
        step = blocks_of(stop - start)
        flat = rows.reshape(rows_n, width)

        def one(i, carry):
            at = pl.multiple_of(start + i * step, tile)
            acc[pl.ds(at, step), :] = dot(dense[pl.ds(at, step), 0:rows_n], flat[...])
            return carry

        lax.fori_loop(0, (stop - start) // step, one, 0)

    def arrived(l, c):
        for j in range(1, group):
            f_copy(l, c, j).wait_recv()

    def unpack(l, c):
        blocks = [f_in[l][c][at] for at in from_at]
        return jnp.concatenate(blocks, axis=0)

    def collect(l, c):
        part = acc[rows_n:, lanes(c)] + dot(dense[rows_n:, rows_n:], hosted[c][...])
        replica[c][...] = part.astype(BF16).reshape(hosts, tile, LANES)
        for j in range(1, group):
            p_out[l][c][j - 1] = replica[c][to_sel[j]]
            p_copy(l, c, j).start()

    split_n = rows_n - own_n

    def with_hosted(at, n):
        return [
            acc[pl.ds(at, n), lanes(c)] + dot(dense[pl.ds(at, n), rows_n:], hosted[c][...])
            for c in range(parts)
        ]

    def own(rows, w_self, w_neigh, emit):
        flat = rows.reshape(rows_n, width)
        step = blocks_of(own_n)

        def one(i, carry):
            at = pl.multiple_of(i * step, step)
            neighbours = jnp.concatenate(with_hosted(at, step), axis=1).astype(BF16)
            emit(
                pl.ds(at, step),
                dot(flat[pl.ds(at, step), :], w_self[...]) + dot(neighbours, w_neigh[...]),
            )
            return carry

        lax.fori_loop(0, own_n // step, one, 0)
        for c, value in enumerate(with_hosted(own_n, split_n)):
            acc[own_n:rows_n, lanes(c)] = value
        return dot(flat[own_n:rows_n, :], w_self[...])

    def receive(l, c):
        for j in range(1, group):
            p_copy(l, c, j).wait_recv()
        for s in range(SPLIT):
            at = own_n + s * tile
            total = acc[at : at + tile, lanes(c)]
            for j in range(1, group):
                total = total + holds[j, s] * p_in[l][c][j - 1].astype(F32)
            total_split[c][s] = total.astype(BF16)

    def split_neigh(c, w_neigh):
        return dot(total_split[c][...].reshape(split_n, LANES), w_neigh[lanes(c), :])

    local(feat, rows_n, slots * tile)
    local(feat, 0, rows_n)
    for c in range(parts):
        arrived(0, c)
        hosted[c][...] = unpack(0, c)
        collect(0, c)

    def keep(at, value):
        first[at, :] = value

    value = own(feat, ws1, wn1, keep)
    before[...] = dot(jnp.concatenate([hosted[c][...] for c in range(parts)], axis=1), ws1[...])
    mine = first[0:own_n, :]
    sums = jnp.sum(mine, axis=0, keepdims=True)
    squares = jnp.sum(mine * mine, axis=0, keepdims=True)

    def totals_of(c):
        return lambda sel: total_split[c][sel]

    for c in range(parts):
        receive(0, c)
        spread(1, c, totals_of(c))
        value = value + split_neigh(c, wn1)
    first[own_n:rows_n, :] = value
    sums = sums + jnp.sum(value, axis=0, keepdims=True)
    squares = squares + jnp.sum(value * value, axis=0, keepdims=True)

    total = jnp.concatenate([sums, squares, jnp.zeros((6, width), F32)], axis=0)
    xy_out[...] = total
    for n in range(len(spots)):
        xy_copy(n).start()
    for n in range(len(spots)):
        xy_copy(n).wait_recv()
        total = total + xy_in[n]
    z_out[...] = total
    for j in range(1, group):
        zs_copy(j).start()
    for j in range(1, group):
        zs_copy(j).wait_recv()
        total = total + z_in[j - 1]
    count = rows_n * nx * ny * group
    mean = total[0:1, :] / count
    var = total[1:2, :] / count - mean * mean
    gain = lax.rsqrt(var + 1e-05) * scale_ref[...]
    shift = shift_ref[...]

    def normal(value):
        return jnp.maximum((value - mean) * gain + shift, 0.0).astype(BF16)

    hidden[...] = normal(first[...]).reshape(rooted, tile, width)
    local(hidden, rows_n, slots * tile)
    for c in range(parts - 1):
        arrived(1, c)
        before[...] += dot(unpack(1, c), wn1[lanes(c), :])
    arrived(1, parts - 1)
    view = normal(before[...] + dot(unpack(1, parts - 1), wn1[lanes(parts - 1), :]))
    for c in range(parts):
        hosted[c][...] = view[:, lanes(c)]
        collect(1, c)

    def finish(at, value):
        out_ref[at, :] = value.astype(BF16)

    local(hidden, 0, rows_n)
    value = own(hidden, ws2, wn2, finish)
    for c in range(parts):
        receive(1, c)
        value = value + split_neigh(c, wn2)
    finish(slice(own_n, rows_n), value)

    for l in range(2):
        for c in range(parts):
            for j in range(1, group):
                f_copy(l, c, j).wait_send()
                p_copy(l, c, j).wait_send()
    for j in range(1, group):
        zs_copy(j).wait_send()
    for n in range(len(spots)):
        xy_copy(n).wait_send()


def per_device(
    features,
    tile_values,
    tile_columns,
    tile_present,
    host_root,
    host_block,
    self_one,
    neigh_one,
    scale_one,
    shift_one,
    self_two,
    neigh_two,
):
    slots, ks, tile, _ = tile_values.shape
    width = features.shape[1]
    rooted = features.shape[0] // tile
    hosts = slots - rooted
    nx, ny, group = (lax.axis_size(name) for name in ("gx", "gy", "gz"))
    peers, spots = group - 1, nx * ny - 1
    parts = width // LANES
    rows_n = rooted * tile
    sizes = (nx, ny, group, slots, ks, tile, width, rooted)

    box = pltpu.VMEM((peers, tile, LANES), BF16)
    dma = pltpu.SemaphoreType.DMA
    scratch = [
        *[pltpu.SMEM(tile_columns.shape, jnp.int32)] * 2,
        *[pltpu.SMEM(host_root.shape, jnp.int32)] * 2,
        pltpu.VMEM((rooted, tile, width), BF16),
        pltpu.VMEM(tile_values.shape, BF16),
        *[pltpu.VMEM((width, width), BF16)] * 4,
        *[pltpu.VMEM((1, width), F32)] * 2,
        pltpu.VMEM((slots * tile, slots * tile), BF16),
        pltpu.VMEM((slots * tile, width), F32),
        pltpu.VMEM((rows_n, width), F32),
        pltpu.VMEM((rooted, tile, width), BF16),
        pltpu.VMEM((hosts * tile, width), F32),
        *[pltpu.VMEM((SPLIT, tile, LANES), BF16)] * parts,
        *[pltpu.VMEM((hosts * tile, LANES), BF16)] * parts,
        *[pltpu.VMEM((hosts, tile, LANES), BF16)] * parts,
        *[box] * (8 * parts),
        pltpu.VMEM((8, width), F32),
        pltpu.VMEM((peers, 8, width), F32),
        pltpu.VMEM((8, width), F32),
        pltpu.VMEM((spots, 8, width), F32),
        dma((13,)),
        *[dma((2, parts, peers))] * 4,
        *[dma((peers,))] * 2,
        *[dma((spots,))] * 2,
    ]
    vmem = pl.BlockSpec(memory_space=pltpu.VMEM)
    hbm = pl.BlockSpec(memory_space=pltpu.HBM)
    call = pl.pallas_call(
        functools.partial(kernel, sizes),
        out_shape=jax.ShapeDtypeStruct((rows_n, width), BF16),
        in_specs=[hbm] * 12,
        out_specs=vmem,
        scratch_shapes=scratch,
        compiler_params=pltpu.CompilerParams(
            collective_id=0, has_side_effects=True, vmem_limit_bytes=40 * 1024 * 1024
        ),
    )
    operands = (
        tile_columns,
        tile_present,
        host_root,
        host_block,
        features.reshape(rooted, tile, width),
        tile_values,
        self_one,
        neigh_one,
        self_two,
        neigh_two,
        scale_one.reshape(1, width),
        shift_one.reshape(1, width),
    )
    return call(*(pltpu.with_memory_space_constraint(x, pltpu.HBM) for x in operands))


def solution(mesh):
    return jax.shard_map(
        per_device,
        mesh=mesh,
        in_specs=(
            P(("gx", "gy", "gz"), None),
            P(("gx", "gy", "gz"), None, None, None),
            P(("gx", "gy", "gz"), None),
            P(("gx", "gy", "gz"), None),
            P(("gx", "gy")),
            P(("gx", "gy")),
            P(),
            P(),
            P(),
            P(),
            P(),
            P(),
        ),
        out_specs=P(("gx", "gy", "gz"), None),
        check_vma=False,
    )
```

```python
import functools

import jax
import jax.numpy as jnp
from jax import lax
from jax.experimental import pallas as pl
from jax.experimental.pallas import tpu as pltpu
from jax.sharding import PartitionSpec as P

OWN = 4
SPLIT = 2
LANES = 128
F32 = jnp.float32
BF16 = jnp.bfloat16


def dot(a, b):
    return jnp.dot(a, b, preferred_element_type=F32)


def kernel(
    sizes,
    columns_hbm,
    present_hbm,
    root_hbm,
    block_hbm,
    features_hbm,
    tiles_hbm,
    self_one_hbm,
    neigh_one_hbm,
    self_two_hbm,
    neigh_two_hbm,
    scale_hbm,
    shift_hbm,
    out_ref,
    *scratch,
):
    nx, ny, group, slots, ks, tile, width, rooted = sizes
    hosts = slots - rooted
    rows_n = rooted * tile
    own_n = OWN * tile
    parts = width // LANES
    peers = group - 1
    scratch = list(scratch)

    def take(n):
        got = scratch[:n]
        del scratch[:n]
        return got

    columns_ref, present_ref, root_ref, block_ref = take(4)
    feat, tiles, ws1, wn1, ws2, wn2, scale_ref, shift_ref = take(8)
    dense, acc, first, hidden, before = take(5)
    total_split = take(parts)
    hosted = take(parts)
    replica = take(parts)
    f_in = [take(parts) for _ in range(2)]
    f_out = [take(parts) for _ in range(2)]
    p_in = [take(parts) for _ in range(2)]
    p_out = [take(parts) for _ in range(2)]
    z_out, z_in, xy_out, xy_in = take(4)
    local_sem, f_send, f_recv, p_send, p_recv, z_send, z_recv, xy_send, xy_recv = take(9)

    gx, gy, gz = lax.axis_index("gx"), lax.axis_index("gy"), lax.axis_index("gz")
    sources = (
        (root_hbm, root_ref),
        (block_hbm, block_ref),
        (features_hbm.at[OWN:], feat.at[OWN:]),
        (columns_hbm, columns_ref),
        (present_hbm, present_ref),
        (tiles_hbm, tiles),
        (features_hbm.at[:OWN], feat.at[:OWN]),
        (self_one_hbm, ws1),
        (neigh_one_hbm, wn1),
        (self_two_hbm, ws2),
        (neigh_two_hbm, wn2),
        (scale_hbm, scale_ref),
        (shift_hbm, shift_ref),
    )
    loads = [
        pltpu.make_async_copy(src, dst, local_sem.at[i]) for i, (src, dst) in enumerate(sources)
    ]

    def wrap(value, size):
        return jnp.where(value >= size, value - size, value)

    def ahead(j):
        return wrap(gz + j, group)

    def behind(j):
        return wrap(gz + group - j, group)

    spots = [(i, k) for i in range(nx) for k in range(ny) if (i, k) != (0, 0)]

    def spot_id(spot):
        return {"gx": wrap(gx + spot[0], nx), "gy": wrap(gy + spot[1], ny)}

    barrier = pltpu.get_barrier_semaphore()
    for j in range(1, group):
        pl.semaphore_signal(
            barrier, inc=1, device_id={"gz": ahead(j)}, device_id_type=pl.DeviceIdType.MESH
        )
    for spot in spots:
        pl.semaphore_signal(
            barrier, inc=1, device_id=spot_id(spot), device_id_type=pl.DeviceIdType.MESH
        )

    for load in loads:
        load.start()

    def z_copy(src, dst, send, recv, j):
        return pltpu.make_async_remote_copy(
            src_ref=src,
            dst_ref=dst,
            send_sem=send,
            recv_sem=recv,
            device_id={"gz": ahead(j)},
            device_id_type=pl.DeviceIdType.MESH,
        )

    def f_copy(l, c, j):
        return z_copy(
            f_out[l][c].at[j - 1], f_in[l][c].at[j - 1], f_send.at[l, c, j - 1], f_recv.at[l, c, j - 1], j
        )

    def p_copy(l, c, j):
        return z_copy(
            p_out[l][c].at[j - 1], p_in[l][c].at[j - 1], p_send.at[l, c, j - 1], p_recv.at[l, c, j - 1], j
        )

    def zs_copy(j):
        return z_copy(z_out, z_in.at[j - 1], z_send.at[j - 1], z_recv.at[j - 1], j)

    def xy_copy(n):
        return pltpu.make_async_remote_copy(
            src_ref=xy_out,
            dst_ref=xy_in.at[n],
            send_sem=xy_send.at[n],
            recv_sem=xy_recv.at[n],
            device_id=spot_id(spots[n]),
            device_id_type=pl.DeviceIdType.MESH,
        )

    def lanes(c):
        return slice(c * LANES, (c + 1) * LANES)

    def wanted(j):
        q = ahead(j)
        sel = jnp.int32(0)
        for h in range(hosts):
            at = q * hosts + h
            sel = jnp.where(root_ref[at] == gz, block_ref[at], sel)
        return sel

    def spread(l, c, block):
        for j in range(1, group):
            f_out[l][c][j - 1] = block(wants[j])
            f_copy(l, c, j).start()

    def split_feature(sel, c):
        block = feat[OWN, :, lanes(c)]
        for s in range(1, SPLIT):
            block = jnp.where(sel == s, feat[OWN + s, :, lanes(c)], block)
        return block

    for load in loads[:2]:
        load.wait()
    wants = {j: wanted(j) for j in range(1, group)}
    my_roots = [root_ref[gz * hosts + h] for h in range(hosts)]
    from_at = []
    for root in my_roots:
        at = wrap(gz - root + group, group) - 1
        from_at.append(jnp.clip(at, 0, peers - 1))
    to_sel = {}
    holds = {}
    for j in range(1, group):
        target, q = ahead(j), behind(j)
        sel = jnp.int32(0)
        for h in range(hosts):
            sel = jnp.where(my_roots[h] == target, h, sel)
        to_sel[j] = sel
        for s in range(SPLIT):
            count = jnp.int32(0)
            for h in range(hosts):
                spot = q * hosts + h
                count = count + jnp.where((root_ref[spot] == gz) & (block_ref[spot] == s), 1, 0)
            holds[j, s] = count.astype(F32)
    loads[2].wait()
    pl.semaphore_wait(barrier, peers + len(spots))
    for c in range(parts):
        spread(0, c, lambda sel: split_feature(sel, c))

    for load in loads[3:6]:
        load.wait()

    def build(b, carry):
        at = pl.multiple_of(b * tile, tile)
        for c in range(slots):
            total = jnp.zeros((tile, tile), BF16)
            for k in range(ks):
                on = (columns_ref[b, k] == c) & (present_ref[b, k] > 0)
                total = total + jnp.where(on, tiles[b, k], jnp.zeros((tile, tile), BF16))
            dense[pl.ds(at, tile), c * tile : (c + 1) * tile] = total
        return carry

    lax.fori_loop(0, slots, build, 0)
    for load in loads[6:]:
        load.wait()

    def blocks_of(n):
        return 2 * tile if n % (2 * tile) == 0 else tile

    def local(rows, start, stop):
        step = blocks_of(stop - start)
        flat = rows.reshape(rows_n, width)

        def one(i, carry):
            at = pl.multiple_of(start + i * step, tile)
            acc[pl.ds(at, step), :] = dot(dense[pl.ds(at, step), 0:rows_n], flat[...])
            return carry

        lax.fori_loop(0, (stop - start) // step, one, 0)

    def arrived(l, c):
        for j in range(1, group):
            f_copy(l, c, j).wait_recv()

    def unpack(l, c):
        blocks = [f_in[l][c][at] for at in from_at]
        return jnp.concatenate(blocks, axis=0)

    def collect(l, c):
        part = acc[rows_n:, lanes(c)] + dot(dense[rows_n:, rows_n:], hosted[c][...])
        replica[c][...] = part.astype(BF16).reshape(hosts, tile, LANES)
        for j in range(1, group):
            p_out[l][c][j - 1] = replica[c][to_sel[j]]
            p_copy(l, c, j).start()

    split_n = rows_n - own_n

    def with_hosted(at, n):
        return [
            acc[pl.ds(at, n), lanes(c)] + dot(dense[pl.ds(at, n), rows_n:], hosted[c][...])
            for c in range(parts)
        ]

    def own(rows, w_self, w_neigh, emit):
        flat = rows.reshape(rows_n, width)
        step = blocks_of(own_n)

        def one(i, carry):
            at = pl.multiple_of(i * step, step)
            neighbours = jnp.concatenate(with_hosted(at, step), axis=1).astype(BF16)
            emit(
                pl.ds(at, step),
                dot(flat[pl.ds(at, step), :], w_self[...]) + dot(neighbours, w_neigh[...]),
            )
            return carry

        lax.fori_loop(0, own_n // step, one, 0)
        for c, value in enumerate(with_hosted(own_n, split_n)):
            acc[own_n:rows_n, lanes(c)] = value
        return dot(flat[own_n:rows_n, :], w_self[...])

    def receive(l, c):
        for j in range(1, group):
            p_copy(l, c, j).wait_recv()
        for s in range(SPLIT):
            at = own_n + s * tile
            total = acc[at : at + tile, lanes(c)]
            for j in range(1, group):
                total = total + holds[j, s] * p_in[l][c][j - 1].astype(F32)
            total_split[c][s] = total.astype(BF16)

    def split_neigh(c, w_neigh):
        return dot(total_split[c][...].reshape(split_n, LANES), w_neigh[lanes(c), :])

    local(feat, rows_n, slots * tile)
    local(feat, 0, rows_n)
    for c in range(parts):
        arrived(0, c)
        hosted[c][...] = unpack(0, c)
        collect(0, c)

    def keep(at, value):
        first[at, :] = value

    value = own(feat, ws1, wn1, keep)
    before[...] = dot(jnp.concatenate([hosted[c][...] for c in range(parts)], axis=1), ws1[...])
    mine = first[0:own_n, :]
    sums = jnp.sum(mine, axis=0, keepdims=True)
    squares = jnp.sum(mine * mine, axis=0, keepdims=True)

    early = lax.rem(gy, 2) == 0

    def totals_of(c):
        return lambda sel: total_split[c][sel]

    for c in range(parts):
        receive(0, c)

        @pl.when(early)
        def _():
            spread(1, c, totals_of(c))

        value = value + split_neigh(c, wn1)
    first[own_n:rows_n, :] = value
    sums = sums + jnp.sum(value, axis=0, keepdims=True)
    squares = squares + jnp.sum(value * value, axis=0, keepdims=True)

    total = jnp.concatenate([sums, squares, jnp.zeros((6, width), F32)], axis=0)
    xy_out[...] = total
    for n in range(len(spots)):
        xy_copy(n).start()
    for n in range(len(spots)):
        xy_copy(n).wait_recv()
        total = total + xy_in[n]
    z_out[...] = total
    for j in range(1, group):
        zs_copy(j).start()

    @pl.when(jnp.logical_not(early))
    def _():
        for c in range(parts):
            spread(1, c, totals_of(c))

    for j in range(1, group):
        zs_copy(j).wait_recv()
        total = total + z_in[j - 1]
    count = rows_n * nx * ny * group
    mean = total[0:1, :] / count
    var = total[1:2, :] / count - mean * mean
    gain = lax.rsqrt(var + 1e-05) * scale_ref[...]
    shift = shift_ref[...]

    def normal(value):
        return jnp.maximum((value - mean) * gain + shift, 0.0).astype(BF16)

    hidden[...] = normal(first[...]).reshape(rooted, tile, width)
    local(hidden, rows_n, slots * tile)
    for c in range(parts - 1):
        arrived(1, c)
        before[...] += dot(unpack(1, c), wn1[lanes(c), :])
    arrived(1, parts - 1)
    view = normal(before[...] + dot(unpack(1, parts - 1), wn1[lanes(parts - 1), :]))
    for c in range(parts):
        hosted[c][...] = view[:, lanes(c)]
        collect(1, c)

    def finish(at, value):
        out_ref[at, :] = value.astype(BF16)

    local(hidden, 0, rows_n)
    value = own(hidden, ws2, wn2, finish)
    for c in range(parts):
        receive(1, c)
        value = value + split_neigh(c, wn2)
    finish(slice(own_n, rows_n), value)

    for l in range(2):
        for c in range(parts):
            for j in range(1, group):
                f_copy(l, c, j).wait_send()
                p_copy(l, c, j).wait_send()
    for j in range(1, group):
        zs_copy(j).wait_send()
    for n in range(len(spots)):
        xy_copy(n).wait_send()


def per_device(
    features,
    tile_values,
    tile_columns,
    tile_present,
    host_root,
    host_block,
    self_one,
    neigh_one,
    scale_one,
    shift_one,
    self_two,
    neigh_two,
):
    slots, ks, tile, _ = tile_values.shape
    width = features.shape[1]
    rooted = features.shape[0] // tile
    hosts = slots - rooted
    nx, ny, group = (lax.axis_size(name) for name in ("gx", "gy", "gz"))
    peers, spots = group - 1, nx * ny - 1
    parts = width // LANES
    rows_n = rooted * tile
    sizes = (nx, ny, group, slots, ks, tile, width, rooted)

    box = pltpu.VMEM((peers, tile, LANES), BF16)
    dma = pltpu.SemaphoreType.DMA
    scratch = [
        *[pltpu.SMEM(tile_columns.shape, jnp.int32)] * 2,
        *[pltpu.SMEM(host_root.shape, jnp.int32)] * 2,
        pltpu.VMEM((rooted, tile, width), BF16),
        pltpu.VMEM(tile_values.shape, BF16),
        *[pltpu.VMEM((width, width), BF16)] * 4,
        *[pltpu.VMEM((1, width), F32)] * 2,
        pltpu.VMEM((slots * tile, slots * tile), BF16),
        pltpu.VMEM((slots * tile, width), F32),
        pltpu.VMEM((rows_n, width), F32),
        pltpu.VMEM((rooted, tile, width), BF16),
        pltpu.VMEM((hosts * tile, width), F32),
        *[pltpu.VMEM((SPLIT, tile, LANES), BF16)] * parts,
        *[pltpu.VMEM((hosts * tile, LANES), BF16)] * parts,
        *[pltpu.VMEM((hosts, tile, LANES), BF16)] * parts,
        *[box] * (8 * parts),
        pltpu.VMEM((8, width), F32),
        pltpu.VMEM((peers, 8, width), F32),
        pltpu.VMEM((8, width), F32),
        pltpu.VMEM((spots, 8, width), F32),
        dma((13,)),
        *[dma((2, parts, peers))] * 4,
        *[dma((peers,))] * 2,
        *[dma((spots,))] * 2,
    ]
    vmem = pl.BlockSpec(memory_space=pltpu.VMEM)
    hbm = pl.BlockSpec(memory_space=pltpu.HBM)
    call = pl.pallas_call(
        functools.partial(kernel, sizes),
        out_shape=jax.ShapeDtypeStruct((rows_n, width), BF16),
        in_specs=[hbm] * 12,
        out_specs=vmem,
        scratch_shapes=scratch,
        compiler_params=pltpu.CompilerParams(
            collective_id=0, has_side_effects=True, vmem_limit_bytes=40 * 1024 * 1024
        ),
    )
    operands = (
        tile_columns,
        tile_present,
        host_root,
        host_block,
        features.reshape(rooted, tile, width),
        tile_values,
        self_one,
        neigh_one,
        self_two,
        neigh_two,
        scale_one.reshape(1, width),
        shift_one.reshape(1, width),
    )
    return call(*(pltpu.with_memory_space_constraint(x, pltpu.HBM) for x in operands))


def solution(mesh):
    return jax.shard_map(
        per_device,
        mesh=mesh,
        in_specs=(
            P(("gx", "gy", "gz"), None),
            P(("gx", "gy", "gz"), None, None, None),
            P(("gx", "gy", "gz"), None),
            P(("gx", "gy", "gz"), None),
            P(("gx", "gy")),
            P(("gx", "gy")),
            P(),
            P(),
            P(),
            P(),
            P(),
            P(),
        ),
        out_specs=P(("gx", "gy", "gz"), None),
        check_vma=False,
    )
```

```python
import functools

import jax
import jax.numpy as jnp
from jax import lax
from jax.experimental import pallas as pl
from jax.experimental.pallas import tpu as pltpu
from jax.sharding import PartitionSpec as P

OWN = 4
SPLIT = 2
LANES = 128
F32 = jnp.float32
BF16 = jnp.bfloat16


def dot(a, b):
    return jnp.dot(a, b, preferred_element_type=F32)


def kernel(
    sizes,
    columns_hbm,
    present_hbm,
    root_hbm,
    block_hbm,
    features_hbm,
    tiles_hbm,
    self_one_hbm,
    neigh_one_hbm,
    self_two_hbm,
    neigh_two_hbm,
    scale_hbm,
    shift_hbm,
    out_ref,
    *scratch,
):
    nx, ny, group, slots, ks, tile, width, rooted = sizes
    hosts = slots - rooted
    rows_n = rooted * tile
    own_n = OWN * tile
    parts = width // LANES
    peers = group - 1
    scratch = list(scratch)

    def take(n):
        got = scratch[:n]
        del scratch[:n]
        return got

    columns_ref, present_ref, root_ref, block_ref = take(4)
    feat, tiles, ws1, wn1, ws2, wn2, scale_ref, shift_ref = take(8)
    dense, acc, first, hidden, before = take(5)
    total_split = take(parts)
    hosted = take(parts)
    replica = take(parts)
    f_in = [take(parts) for _ in range(2)]
    f_out = [take(parts) for _ in range(2)]
    p_in = [take(parts) for _ in range(2)]
    p_out = [take(parts) for _ in range(2)]
    z_out, z_in, xy_out, xy_in = take(4)
    local_sem, f_send, f_recv, p_send, p_recv, z_send, z_recv, xy_send, xy_recv = take(9)

    gx, gy, gz = lax.axis_index("gx"), lax.axis_index("gy"), lax.axis_index("gz")
    sources = (
        (root_hbm, root_ref),
        (block_hbm, block_ref),
        (features_hbm.at[OWN:], feat.at[OWN:]),
        (columns_hbm, columns_ref),
        (present_hbm, present_ref),
        (tiles_hbm, tiles),
        (features_hbm.at[:OWN], feat.at[:OWN]),
        (self_one_hbm, ws1),
        (neigh_one_hbm, wn1),
        (self_two_hbm, ws2),
        (neigh_two_hbm, wn2),
        (scale_hbm, scale_ref),
        (shift_hbm, shift_ref),
    )
    loads = [
        pltpu.make_async_copy(src, dst, local_sem.at[i]) for i, (src, dst) in enumerate(sources)
    ]

    def wrap(value, size):
        return jnp.where(value >= size, value - size, value)

    def ahead(j):
        return wrap(gz + j, group)

    def behind(j):
        return wrap(gz + group - j, group)

    spots = [(i, k) for i in range(nx) for k in range(ny) if (i, k) != (0, 0)]

    def spot_id(spot):
        return {"gx": wrap(gx + spot[0], nx), "gy": wrap(gy + spot[1], ny)}

    barrier = pltpu.get_barrier_semaphore()
    for j in range(1, group):
        pl.semaphore_signal(
            barrier, inc=1, device_id={"gz": ahead(j)}, device_id_type=pl.DeviceIdType.MESH
        )
    for spot in spots:
        pl.semaphore_signal(
            barrier, inc=1, device_id=spot_id(spot), device_id_type=pl.DeviceIdType.MESH
        )

    for load in loads:
        load.start()

    def z_copy(src, dst, send, recv, j):
        return pltpu.make_async_remote_copy(
            src_ref=src,
            dst_ref=dst,
            send_sem=send,
            recv_sem=recv,
            device_id={"gz": ahead(j)},
            device_id_type=pl.DeviceIdType.MESH,
        )

    def f_copy(l, c, j):
        return z_copy(
            f_out[l][c].at[j - 1], f_in[l][c].at[j - 1], f_send.at[l, c, j - 1], f_recv.at[l, c, j - 1], j
        )

    def p_copy(l, c, j):
        return z_copy(
            p_out[l][c].at[j - 1], p_in[l][c].at[j - 1], p_send.at[l, c, j - 1], p_recv.at[l, c, j - 1], j
        )

    def zs_copy(j):
        return z_copy(z_out, z_in.at[j - 1], z_send.at[j - 1], z_recv.at[j - 1], j)

    def xy_copy(n):
        return pltpu.make_async_remote_copy(
            src_ref=xy_out,
            dst_ref=xy_in.at[n],
            send_sem=xy_send.at[n],
            recv_sem=xy_recv.at[n],
            device_id=spot_id(spots[n]),
            device_id_type=pl.DeviceIdType.MESH,
        )

    def lanes(c):
        return slice(c * LANES, (c + 1) * LANES)

    def wanted(j):
        q = ahead(j)
        sel = jnp.int32(0)
        for h in range(hosts):
            at = q * hosts + h
            sel = jnp.where(root_ref[at] == gz, block_ref[at], sel)
        return sel

    def spread(l, c, block):
        for j in range(1, group):
            f_out[l][c][j - 1] = block(wants[j])
            f_copy(l, c, j).start()

    def split_feature(sel, c):
        block = feat[OWN, :, lanes(c)]
        for s in range(1, SPLIT):
            block = jnp.where(sel == s, feat[OWN + s, :, lanes(c)], block)
        return block

    for load in loads[:2]:
        load.wait()
    wants = {j: wanted(j) for j in range(1, group)}
    my_roots = [root_ref[gz * hosts + h] for h in range(hosts)]
    from_at = []
    for root in my_roots:
        at = wrap(gz - root + group, group) - 1
        from_at.append(jnp.clip(at, 0, peers - 1))
    to_sel = {}
    holds = {}
    for j in range(1, group):
        target, q = ahead(j), behind(j)
        sel = jnp.int32(0)
        for h in range(hosts):
            sel = jnp.where(my_roots[h] == target, h, sel)
        to_sel[j] = sel
        for s in range(SPLIT):
            count = jnp.int32(0)
            for h in range(hosts):
                spot = q * hosts + h
                count = count + jnp.where((root_ref[spot] == gz) & (block_ref[spot] == s), 1, 0)
            holds[j, s] = count.astype(F32)
    loads[2].wait()
    pl.semaphore_wait(barrier, peers + len(spots))
    for c in range(parts):
        spread(0, c, lambda sel: split_feature(sel, c))

    for load in loads[3:6]:
        load.wait()

    def build(b, carry):
        at = pl.multiple_of(b * tile, tile)
        for c in range(slots):
            total = jnp.zeros((tile, tile), BF16)
            for k in range(ks):
                on = (columns_ref[b, k] == c) & (present_ref[b, k] > 0)
                total = total + jnp.where(on, tiles[b, k], jnp.zeros((tile, tile), BF16))
            dense[pl.ds(at, tile), c * tile : (c + 1) * tile] = total
        return carry

    lax.fori_loop(0, slots, build, 0)
    for load in loads[6:]:
        load.wait()

    def blocks_of(n):
        return 2 * tile if n % (2 * tile) == 0 else tile

    def local(rows, start, stop):
        step = blocks_of(stop - start)
        flat = rows.reshape(rows_n, width)

        def one(i, carry):
            at = pl.multiple_of(start + i * step, tile)
            acc[pl.ds(at, step), :] = dot(dense[pl.ds(at, step), 0:rows_n], flat[...])
            return carry

        lax.fori_loop(0, (stop - start) // step, one, 0)

    def arrived(l, c):
        for j in range(1, group):
            f_copy(l, c, j).wait_recv()

    def unpack(l, c):
        blocks = [f_in[l][c][at] for at in from_at]
        return jnp.concatenate(blocks, axis=0)

    def collect(l, c):
        part = acc[rows_n:, lanes(c)] + dot(dense[rows_n:, rows_n:], hosted[c][...])
        replica[c][...] = part.astype(BF16).reshape(hosts, tile, LANES)
        for j in range(1, group):
            p_out[l][c][j - 1] = replica[c][to_sel[j]]
            p_copy(l, c, j).start()

    split_n = rows_n - own_n

    def with_hosted(at, n):
        return [
            acc[pl.ds(at, n), lanes(c)] + dot(dense[pl.ds(at, n), rows_n:], hosted[c][...])
            for c in range(parts)
        ]

    def own(rows, w_self, w_neigh, emit):
        flat = rows.reshape(rows_n, width)
        step = blocks_of(own_n)

        def one(i, carry):
            at = pl.multiple_of(i * step, step)
            neighbours = jnp.concatenate(with_hosted(at, step), axis=1).astype(BF16)
            emit(
                pl.ds(at, step),
                dot(flat[pl.ds(at, step), :], w_self[...]) + dot(neighbours, w_neigh[...]),
            )
            return carry

        lax.fori_loop(0, own_n // step, one, 0)
        for c, value in enumerate(with_hosted(own_n, split_n)):
            acc[own_n:rows_n, lanes(c)] = value
        return dot(flat[own_n:rows_n, :], w_self[...])

    def receive(l, c):
        for j in range(1, group):
            p_copy(l, c, j).wait_recv()
        for s in range(SPLIT):
            at = own_n + s * tile
            total = acc[at : at + tile, lanes(c)]
            for j in range(1, group):
                total = total + holds[j, s] * p_in[l][c][j - 1].astype(F32)
            total_split[c][s] = total.astype(BF16)

    def split_neigh(c, w_neigh):
        return dot(total_split[c][...].reshape(split_n, LANES), w_neigh[lanes(c), :])

    local(feat, rows_n, slots * tile)
    local(feat, 0, rows_n)
    for c in range(parts):
        arrived(0, c)
        hosted[c][...] = unpack(0, c)
        collect(0, c)

    def keep(at, value):
        first[at, :] = value

    value = own(feat, ws1, wn1, keep)
    before[...] = dot(jnp.concatenate([hosted[c][...] for c in range(parts)], axis=1), ws1[...])
    mine = first[0:own_n, :]
    sums = jnp.sum(mine, axis=0, keepdims=True)
    squares = jnp.sum(mine * mine, axis=0, keepdims=True)

    early = lax.rem(gy, 2) == 0

    def totals_of(c):
        return lambda sel: total_split[c][sel]

    for c in range(parts):
        receive(0, c)

        @pl.when(early)
        def _():
            spread(1, c, totals_of(c))

        value = value + split_neigh(c, wn1)
    first[own_n:rows_n, :] = value
    sums = sums + jnp.sum(value, axis=0, keepdims=True)
    squares = squares + jnp.sum(value * value, axis=0, keepdims=True)

    total = jnp.concatenate([sums, squares, jnp.zeros((6, width), F32)], axis=0)
    xy_out[...] = total
    for n in range(len(spots)):
        xy_copy(n).start()

    @pl.when(jnp.logical_not(early))
    def _():
        for c in range(parts):
            spread(1, c, totals_of(c))

    for n in range(len(spots)):
        xy_copy(n).wait_recv()
        total = total + xy_in[n]
    z_out[...] = total
    for j in range(1, group):
        zs_copy(j).start()

    for j in range(1, group):
        zs_copy(j).wait_recv()
        total = total + z_in[j - 1]
    count = rows_n * nx * ny * group
    mean = total[0:1, :] / count
    var = total[1:2, :] / count - mean * mean
    gain = lax.rsqrt(var + 1e-05) * scale_ref[...]
    shift = shift_ref[...]

    def normal(value):
        return jnp.maximum((value - mean) * gain + shift, 0.0).astype(BF16)

    hidden[...] = normal(first[...]).reshape(rooted, tile, width)
    local(hidden, rows_n, slots * tile)
    for c in range(parts - 1):
        arrived(1, c)
        before[...] += dot(unpack(1, c), wn1[lanes(c), :])
    arrived(1, parts - 1)
    view = normal(before[...] + dot(unpack(1, parts - 1), wn1[lanes(parts - 1), :]))
    for c in range(parts):
        hosted[c][...] = view[:, lanes(c)]
        collect(1, c)

    def finish(at, value):
        out_ref[at, :] = value.astype(BF16)

    local(hidden, 0, rows_n)
    value = own(hidden, ws2, wn2, finish)
    for c in range(parts):
        receive(1, c)
        value = value + split_neigh(c, wn2)
    finish(slice(own_n, rows_n), value)

    for l in range(2):
        for c in range(parts):
            for j in range(1, group):
                f_copy(l, c, j).wait_send()
                p_copy(l, c, j).wait_send()
    for j in range(1, group):
        zs_copy(j).wait_send()
    for n in range(len(spots)):
        xy_copy(n).wait_send()


def per_device(
    features,
    tile_values,
    tile_columns,
    tile_present,
    host_root,
    host_block,
    self_one,
    neigh_one,
    scale_one,
    shift_one,
    self_two,
    neigh_two,
):
    slots, ks, tile, _ = tile_values.shape
    width = features.shape[1]
    rooted = features.shape[0] // tile
    hosts = slots - rooted
    nx, ny, group = (lax.axis_size(name) for name in ("gx", "gy", "gz"))
    peers, spots = group - 1, nx * ny - 1
    parts = width // LANES
    rows_n = rooted * tile
    sizes = (nx, ny, group, slots, ks, tile, width, rooted)

    box = pltpu.VMEM((peers, tile, LANES), BF16)
    dma = pltpu.SemaphoreType.DMA
    scratch = [
        *[pltpu.SMEM(tile_columns.shape, jnp.int32)] * 2,
        *[pltpu.SMEM(host_root.shape, jnp.int32)] * 2,
        pltpu.VMEM((rooted, tile, width), BF16),
        pltpu.VMEM(tile_values.shape, BF16),
        *[pltpu.VMEM((width, width), BF16)] * 4,
        *[pltpu.VMEM((1, width), F32)] * 2,
        pltpu.VMEM((slots * tile, slots * tile), BF16),
        pltpu.VMEM((slots * tile, width), F32),
        pltpu.VMEM((rows_n, width), F32),
        pltpu.VMEM((rooted, tile, width), BF16),
        pltpu.VMEM((hosts * tile, width), F32),
        *[pltpu.VMEM((SPLIT, tile, LANES), BF16)] * parts,
        *[pltpu.VMEM((hosts * tile, LANES), BF16)] * parts,
        *[pltpu.VMEM((hosts, tile, LANES), BF16)] * parts,
        *[box] * (8 * parts),
        pltpu.VMEM((8, width), F32),
        pltpu.VMEM((peers, 8, width), F32),
        pltpu.VMEM((8, width), F32),
        pltpu.VMEM((spots, 8, width), F32),
        dma((13,)),
        *[dma((2, parts, peers))] * 4,
        *[dma((peers,))] * 2,
        *[dma((spots,))] * 2,
    ]
    vmem = pl.BlockSpec(memory_space=pltpu.VMEM)
    hbm = pl.BlockSpec(memory_space=pltpu.HBM)
    call = pl.pallas_call(
        functools.partial(kernel, sizes),
        out_shape=jax.ShapeDtypeStruct((rows_n, width), BF16),
        in_specs=[hbm] * 12,
        out_specs=vmem,
        scratch_shapes=scratch,
        compiler_params=pltpu.CompilerParams(
            collective_id=0, has_side_effects=True, vmem_limit_bytes=40 * 1024 * 1024
        ),
    )
    operands = (
        tile_columns,
        tile_present,
        host_root,
        host_block,
        features.reshape(rooted, tile, width),
        tile_values,
        self_one,
        neigh_one,
        self_two,
        neigh_two,
        scale_one.reshape(1, width),
        shift_one.reshape(1, width),
    )
    return call(*(pltpu.with_memory_space_constraint(x, pltpu.HBM) for x in operands))


def solution(mesh):
    return jax.shard_map(
        per_device,
        mesh=mesh,
        in_specs=(
            P(("gx", "gy", "gz"), None),
            P(("gx", "gy", "gz"), None, None, None),
            P(("gx", "gy", "gz"), None),
            P(("gx", "gy", "gz"), None),
            P(("gx", "gy")),
            P(("gx", "gy")),
            P(),
            P(),
            P(),
            P(),
            P(),
            P(),
        ),
        out_specs=P(("gx", "gy", "gz"), None),
        check_vma=False,
    )
```
